32 devices in a mesh: parts: 2 (over y), pool: 4 (over z), tp: 4 (over x, core).
Axes of the slice: x: 2, y: 2, z: 4, core: 2. Of those that a mesh axis runs over, the one named last changes fastest.
Arguments:
- queries: bfloat16 [4096, 8192], P(('parts', 'pool'), 'tp'), parts along dimension 0, may hold values from -400 to 400
- suffix_kv: bfloat16 [2, 8, 4096, 128], P(None, 'tp', ('parts', 'pool')), parts along dimension 2, may hold values from -12 to 12
- pool_kv: bfloat16 [2, 8, 64, 128, 128], P(None, 'tp', ('parts', 'pool')), parts along dimension 2, may hold values from -6 to 6
- prefix_pages: int32 [8], P('parts'), parts along dimension 0, may hold values from 1 to 4, as said below
- owner_start: int32 [8], P('parts'), parts along dimension 0, may hold values from 0 to 3
- page_slot: int32 [8, 4, 2], P('parts'), parts along dimension 0, may hold values from 0 to 7, as said below
Outputs:
- attention: bfloat16 [4096, 8192], P(('parts', 'pool'), 'tp'), parts along dimension 0
- new_pool: bfloat16 [2, 8, 64, 128, 128], P(None, 'tp', ('parts', 'pool')), parts along dimension 2
The draws below stay inside these ranges and needn't reach their ends.
There are 2 independent parts, one for each index of `parts`. The reference program is written for one: setup_inputs(seed, part) draws one part's arguments, and reference() takes and returns one part's arrays. A program takes and returns all parts, laid end to end along the dimension named above; each array names one. Nothing has to cross between parts.
Inputs may be any that keep to these rules, and one draw needn't show every extreme that they name: For each owner o, the entries page_slot[:, o, :] name each of its 8 slots exactly once. `prefix_pages`: among the 4 requests of one serving group, at least one has exactly 4 prefix pages.
All inputs are finite; a program needn't handle non-finite values.
Results may differ from the reference program's by a relative error of at most 0.0035.
Values may be sent and summed in bfloat16 or wider, within the bound.
No kernel may reach another device: no remote copies, remote signals or barrier semaphores. Data moves between devices by JAX's collectives and lax.ppermute only.
A program may use at most 128 MiB of HBM per device.

```python
import math
import jax
import jax.numpy as jnp
from jax import lax

KVH = 8
HD = 128
GROUP = 8
PAGE = 128
CAP = 2
SUF = 512
REQS = 4
SLOTS = 8
MAXP = 8
SP = 4
POOL_PAGES = 32
N_POOL = 4


def joint_draw(key):
    base_key = jax.random.fold_in(key, 4242)
    key_query, key_cache = jax.random.split(base_key, 2)
    queries = jnp.clip(2.5 * jax.random.normal(key_query, (REQS * SUF, KVH * GROUP * HD), jnp.float32), -15.0, 15.0)
    cache = jnp.clip(jax.random.normal(key_cache, (2, KVH, REQS * SUF, HD), jnp.float32), -6.0, 6.0)
    return (queries, cache)


def draw_queries(key, part):
    return joint_draw(key)[0].astype(jnp.bfloat16)


def draw_suffix_kv(key, part):
    return joint_draw(key)[1].astype(jnp.bfloat16)


def draw_prefix_pages(key, part):
    length_key, pick_key = jax.random.split(jax.random.fold_in(key, 517))
    longest = MAXP - SP
    lengths = jax.random.randint(length_key, (REQS,), 1, longest + 1, dtype=jnp.int32)
    chosen = jax.random.randint(pick_key, (), 0, REQS, dtype=jnp.int32)
    places = jnp.arange(REQS, dtype=jnp.int32)
    return jnp.where(places == chosen, longest, lengths).astype(jnp.int32)


def owner_order(owner_key):
    return jax.random.permutation(owner_key, REQS * CAP).astype(jnp.int32)


def draw_page_slot(key, part):
    owner_keys = jax.random.split(jax.random.fold_in(key, 99), N_POOL)
    orders = jax.vmap(owner_order)(owner_keys).reshape(N_POOL, REQS, CAP)
    return jnp.transpose(orders, (1, 0, 2)).astype(jnp.int32)


def plant(array, rng, low, top_value):
    spot = [jax.random.randint(jax.random.fold_in(rng, axis), (), 0, length) for axis, length in enumerate(array.shape)]
    main_axis = array.shape.index(max(array.shape))
    neighbour = spot[:main_axis] + [(spot[main_axis] + 1) % array.shape[main_axis]] + spot[main_axis + 1:]
    return array.at[tuple(spot)].set(low).at[tuple(neighbour)].set(top_value)


def block_scale(rng, extent, cuts, smallest, largest):
    def one(position, parts):
        steps = jax.random.uniform(jax.random.fold_in(jax.random.fold_in(rng, 6), position), (parts,), jnp.float32, smallest / len(cuts), largest / len(cuts))
        return jnp.repeat(jnp.exp(steps), extent[position] // parts).reshape((-1,) + (1,) * (len(extent) - position - 1))

    gain = one(*cuts[0])
    for cut in cuts[1:]:
        gain = gain * one(*cut)
    return gain


def noise(own_key, extent, width, limit, pieces=(), kind=jnp.bfloat16):
    result = width * jax.random.normal(own_key, extent, jnp.float32)
    if pieces:
        result = result * block_scale(own_key, extent, pieces, -0.22, 0.18)
    return jnp.clip(result, -limit, limit).astype(kind)


def setup_inputs(seed: int = 0, part: int = 0) -> dict:
    key_of = jax.random.split(jax.random.key(seed), 7)
    own_keys = jax.random.split(jax.random.fold_in(key_of[6], part), 7)
    queries = draw_queries(jax.random.fold_in(jax.random.fold_in(key_of[6], part), 71), part)
    suffix_kv = draw_suffix_kv(jax.random.fold_in(jax.random.fold_in(key_of[6], part), 71), part)
    pool_kv = noise(own_keys[2], (2, KVH, POOL_PAGES, PAGE, HD), 1.0, 6.0, ((1, 4), (2, 4)))
    prefix_pages = draw_prefix_pages(jax.random.fold_in(jax.random.fold_in(key_of[6], part), 71), part)
    owner_start = plant(jax.random.randint(own_keys[4], (REQS,), 0, N_POOL), jax.random.fold_in(own_keys[4], 1), 0, N_POOL - 1).astype(jnp.int32)
    page_slot = draw_page_slot(jax.random.fold_in(jax.random.fold_in(key_of[6], part), 71), part)
    return dict(queries=queries, suffix_kv=suffix_kv, pool_kv=pool_kv, prefix_pages=prefix_pages, owner_start=owner_start, page_slot=page_slot)


def page_rows(prefix_pages, owner_start, page_slot):
    numbers = jnp.arange(MAXP, dtype=jnp.int32)
    owner_ids = jnp.mod(owner_start[:, None] + numbers[None, :], N_POOL).astype(jnp.int32)
    level_ids = jnp.broadcast_to(numbers[None, :] // N_POOL, owner_ids.shape)
    request_ids = jnp.broadcast_to(jnp.arange(REQS, dtype=jnp.int32)[:, None], owner_ids.shape)
    return (owner_ids * SLOTS + page_slot[request_ids, owner_ids, level_ids]).astype(jnp.int32)

def reference(queries, suffix_kv, pool_kv, prefix_pages, owner_start, page_slot):
    rows_table = page_rows(prefix_pages, owner_start, page_slot)
    score_scale = 1.0 / math.sqrt(HD)
    page_ids = jnp.arange(MAXP * PAGE, dtype=jnp.int32) // PAGE
    causal = lax.broadcasted_iota(jnp.int32, (SUF, SUF), 1) <= lax.broadcasted_iota(jnp.int32, (SUF, SUF), 0)

    def per_request(request):
        gathered = jnp.take(pool_kv, rows_table[request], axis=2)
        prefix_rows = gathered.reshape(2, KVH, MAXP * PAGE, HD)
        own_rows = lax.dynamic_slice_in_dim(suffix_kv, (request * SUF).astype(jnp.int32), SUF, 2)
        context = jnp.concatenate([prefix_rows, own_rows], axis=2)
        query_rows = lax.dynamic_slice_in_dim(queries, (request * SUF).astype(jnp.int32), SUF, 0)
        query_rows = query_rows.reshape(SUF, KVH, GROUP, HD)
        prefix_seen = page_ids < prefix_pages[request]
        visible = jnp.concatenate([jnp.broadcast_to(prefix_seen[None, :], (SUF, MAXP * PAGE)), causal], axis=1)

        def per_head(kv_head):
            pair = lax.dynamic_index_in_dim(context, kv_head, 1, keepdims=False)
            key_rows = pair[0].astype(jnp.float32)
            value_rows = pair[1].astype(jnp.float32)
            heads_query = lax.dynamic_index_in_dim(query_rows, kv_head, 1, keepdims=False).astype(jnp.float32)
            scores = jnp.einsum('qgd,kd->gqk', heads_query, key_rows) * score_scale
            scores = jnp.where(visible[None], scores, -jnp.inf)
            row_max = lax.optimization_barrier(jnp.max(scores, axis=-1, keepdims=True))
            weights = jnp.exp(scores - row_max)
            weight_sum = lax.optimization_barrier(jnp.sum(weights, axis=-1))
            rounded = lax.optimization_barrier(weights.astype(jnp.bfloat16)).astype(jnp.float32)
            mixed_rows = jnp.einsum('gqk,kd->qgd', rounded, value_rows)
            return mixed_rows / jnp.transpose(weight_sum)[:, :, None]
        heads_out = lax.map(per_head, jnp.arange(KVH, dtype=jnp.int32))
        return jnp.transpose(heads_out, (1, 0, 2, 3)).reshape(SUF, KVH * GROUP * HD).astype(jnp.bfloat16)
    attention = lax.map(per_request, jnp.arange(REQS, dtype=jnp.int32)).reshape(REQS * SUF, KVH * GROUP * HD)
    offsets = jnp.arange(SP, dtype=jnp.int32)
    numbers = prefix_pages[:, None] + offsets[None, :]
    owner_ids = jnp.mod(owner_start[:, None] + numbers, N_POOL).astype(jnp.int32)
    request_ids = jnp.broadcast_to(jnp.arange(REQS, dtype=jnp.int32)[:, None], owner_ids.shape)
    targets = owner_ids * SLOTS + page_slot[request_ids, owner_ids, numbers // N_POOL]
    fresh_pages = suffix_kv.reshape(2, KVH, REQS * SP, PAGE, HD)
    new_pool = pool_kv.at[:, :, targets.reshape(-1).astype(jnp.int32)].set(fresh_pages)
    return (attention, new_pool)
```

```python
import functools
import math

import jax
import jax.numpy as jnp
from jax import lax
from jax.experimental import pallas as pl
from jax.experimental.pallas import tpu as pltpu
from jax.sharding import PartitionSpec as P

HBM = pl.BlockSpec(memory_space=pl.ANY)
SMEM = pl.BlockSpec(memory_space=pltpu.SMEM)
TILE = 256


def fetch_kernel(slots_ref, pool_ref, send_ref, sems):
    groups, levels = send_ref.shape[:2]
    me = lax.axis_index("pool")
    copies = []
    for dest in range(groups):
        for level in range(levels):
            slot = slots_ref[dest, me, level]
            copies.append(
                pltpu.make_async_copy(
                    pool_ref.at[:, :, slot], send_ref.at[dest, level], sems.at[dest, level]
                )
            )
    for copy in copies:
        copy.start()
    for copy in copies:
        copy.wait()


def back_kernel(length_ref, start_ref, suffix_ref, send_ref, sems):
    groups = send_ref.shape[0]
    pages = suffix_ref.shape[2]
    me = lax.axis_index("pool")
    first = start_ref[me] + length_ref[me]

    def each(act):
        for dest in range(groups):
            offset = lax.rem(dest + 4 * groups - lax.rem(first, groups), groups)

            @pl.when(offset < pages)
            def _():
                act(
                    pltpu.make_async_copy(
                        suffix_ref.at[:, :, jnp.minimum(offset, pages - 1)],
                        send_ref.at[dest],
                        sems.at[dest],
                    )
                )

    each(lambda copy: copy.start())
    each(lambda copy: copy.wait())


def place_kernel(pages, length_ref, start_ref, slots_ref, back_ref, pool_ref, new_ref, sems):
    del pool_ref
    requests, groups, levels = slots_ref.shape
    me = lax.axis_index("pool")

    def each(act):
        for request in range(requests):
            length = length_ref[request]
            offset = lax.rem(me + 4 * groups - lax.rem(start_ref[request] + length, groups), groups)

            @pl.when(offset < pages)
            def _():
                level = jnp.minimum(lax.div(length + offset, groups), levels - 1)
                slot = slots_ref[request, me, level]
                act(
                    pltpu.make_async_copy(
                        back_ref.at[request], new_ref.at[:, :, slot], sems.at[request]
                    )
                )

    each(lambda copy: copy.start())
    each(lambda copy: copy.wait())


def attend_kernel(
    scale,
    per_step,
    length_ref,
    start_ref,
    query_ref,
    suffix_ref,
    page_ref,
    pool_ref,
    out_ref,
    new_ref,
    keys,
    values,
    sem,
):
    groups, levels = page_ref.shape[:2]
    page_len, head_dim = page_ref.shape[4:]
    suffix = query_ref.shape[0]
    steps = pl.num_programs(1)
    head, step = pl.program_id(0), pl.program_id(1)
    me = lax.axis_index("pool")
    copy = pltpu.make_async_copy(pool_ref, new_ref, sem)

    @pl.when((head == 0) & (step == 0))
    def _():
        copy.start()

    @pl.when(step == 0)
    def _():
        length, first = length_ref[me], start_ref[me]
        keys[pl.ds(0, suffix), :] = suffix_ref[0, 0]
        values[pl.ds(0, suffix), pl.ds(0, head_dim)] = suffix_ref[1, 0]
        values[pl.ds(0, suffix), pl.ds(head_dim, head_dim)] = jnp.ones(
            (suffix, head_dim), values.dtype
        )
        for owner in range(groups):
            for level in range(levels):
                row = suffix + (owner * levels + level) * page_len
                number = level * groups + lax.rem(owner + groups - first, groups)
                seen = number < length
                key_owner = jnp.where(seen, owner, first)
                key_level = jnp.where(seen, level, 0)
                keys[pl.ds(row, page_len), :] = page_ref[key_owner, key_level, 0, 0]

                @pl.when(seen)
                def _():
                    values[pl.ds(row, page_len), pl.ds(0, head_dim)] = page_ref[owner, level, 1, 0]
                    values[pl.ds(row, page_len), pl.ds(head_dim, head_dim)] = jnp.ones(
                        (page_len, head_dim), values.dtype
                    )

                @pl.when(jnp.logical_not(seen))
                def _():
                    values[pl.ds(row, page_len), :] = jnp.zeros(
                        (page_len, 2 * head_dim), values.dtype
                    )

    tile = min(TILE, suffix)
    total = keys.shape[0]
    seen = lax.broadcasted_iota(jnp.int32, (tile, tile), 1) <= lax.broadcasted_iota(
        jnp.int32, (tile, tile), 0
    )
    contract = (((1,), (1,)), ((), ()))
    dot = functools.partial(lax.dot_general, preferred_element_type=jnp.float32)
    plain = (((1,), (0,)), ((), ()))
    for column in range(per_step):
        lanes = pl.ds(column * head_dim, head_dim)
        for row in range(0, suffix, tile):
            query = query_ref[pl.ds(row, tile), lanes]
            parts = [
                (
                    jnp.where(
                        seen, dot(query, keys[pl.ds(row, tile), :], contract), -jnp.inf
                    ),
                    values[pl.ds(row, tile), :],
                )
            ]
            if row:
                parts.append((dot(query, keys[pl.ds(0, row), :], contract), values[pl.ds(0, row), :]))
            parts.append(
                (
                    dot(query, keys[pl.ds(suffix, total - suffix), :], contract),
                    values[pl.ds(suffix, total - suffix), :],
                )
            )
            top = functools.reduce(
                jnp.maximum, [jnp.max(score, axis=1, keepdims=True) for score, _ in parts]
            )
            mixed = None
            for score, value in parts:
                weight = jnp.exp2((score - top) * scale).astype(jnp.bfloat16)
                part = dot(weight, value, plain)
                mixed = part if mixed is None else mixed + part
            out_ref[pl.ds(row, tile), lanes] = (
                mixed[:, :head_dim] / mixed[:, head_dim:]
            ).astype(out_ref.dtype)

    @pl.when((head == pl.num_programs(0) - 1) & (step == steps - 1))
    def _():
        copy.wait()


def body(queries, suffix_kv, pool_kv, prefix_pages, owner_start, page_slot):
    _, heads, slots, page_len, head_dim = pool_kv.shape
    requests, groups, levels = page_slot.shape
    suffix = queries.shape[0]
    per_kv = queries.shape[1] // (heads * head_dim)
    pages = suffix // page_len
    fetched = -(-(levels * groups - pages) // groups)
    page = (2, heads, page_len, head_dim)
    dtype = pool_kv.dtype

    send = pl.pallas_call(
        fetch_kernel,
        out_shape=jax.ShapeDtypeStruct((groups, fetched) + page, dtype),
        in_specs=[SMEM, HBM],
        out_specs=HBM,
        scratch_shapes=[pltpu.SemaphoreType.DMA((groups, fetched))],
        name="gather_pages",
    )(page_slot, pool_kv)
    received = lax.all_to_all(send, "pool", split_axis=0, concat_axis=0, tiled=True)

    back_send = pl.pallas_call(
        back_kernel,
        out_shape=jax.ShapeDtypeStruct((groups,) + page, dtype),
        in_specs=[SMEM, SMEM, HBM],
        out_specs=HBM,
        scratch_shapes=[pltpu.SemaphoreType.DMA((groups,))],
        name="pick_suffix",
    )(prefix_pages, owner_start, suffix_kv.reshape(2, heads, pages, page_len, head_dim))
    returned = lax.all_to_all(back_send, "pool", split_axis=0, concat_axis=0, tiled=True)

    per_step = math.gcd(per_kv, 4)
    steps = per_kv // per_step
    total = suffix + fetched * groups * page_len
    result, new_pool = pl.pallas_call(
        functools.partial(attend_kernel, math.log2(math.e) / math.sqrt(head_dim), per_step),
        grid=(heads, steps),
        out_shape=(
            jax.ShapeDtypeStruct(queries.shape, dtype),
            jax.ShapeDtypeStruct(pool_kv.shape, dtype),
        ),
        in_specs=[
            SMEM,
            SMEM,
            pl.BlockSpec((suffix, per_step * head_dim), lambda h, s: (0, h * steps + s)),
            pl.BlockSpec((2, 1, suffix, head_dim), lambda h, s: (0, h, 0, 0)),
            pl.BlockSpec(
                (groups, fetched, 2, 1, page_len, head_dim), lambda h, s: (0, 0, 0, h, 0, 0)
            ),
            HBM,
        ],
        out_specs=(
            pl.BlockSpec((suffix, per_step * head_dim), lambda h, s: (0, h * steps + s)),
            HBM,
        ),
        scratch_shapes=[
            pltpu.VMEM((total, head_dim), dtype),
            pltpu.VMEM((total, 2 * head_dim), dtype),
            pltpu.SemaphoreType.DMA(()),
        ],
        compiler_params=pltpu.CompilerParams(vmem_limit_bytes=48 * 1024 * 1024),
        cost_estimate=pl.CostEstimate(
            flops=4 * heads * per_kv * suffix * total * head_dim,
            bytes_accessed=4 * queries.size + 8 * pool_kv.size,
            transcendentals=heads * per_kv * suffix * total,
        ),
        name="attend",
    )(prefix_pages, owner_start, queries, suffix_kv, received, pool_kv)

    new_pool = pl.pallas_call(
        functools.partial(place_kernel, pages),
        out_shape=jax.ShapeDtypeStruct(pool_kv.shape, dtype),
        in_specs=[SMEM, SMEM, SMEM, HBM, HBM],
        out_specs=HBM,
        input_output_aliases={4: 0},
        scratch_shapes=[pltpu.SemaphoreType.DMA((requests,))],
        name="place_pages",
    )(prefix_pages, owner_start, page_slot, returned, new_pool)
    return (result, new_pool)


def solution(mesh):
    in_specs = (
        P(("parts", "pool"), "tp"),
        P(None, "tp", ("parts", "pool"), None),
        P(None, "tp", ("parts", "pool"), None, None),
        P("parts"),
        P("parts"),
        P("parts", None, None),
    )
    out_specs = (P(("parts", "pool"), "tp"), P(None, "tp", ("parts", "pool"), None, None))
    return jax.shard_map(body, mesh=mesh, in_specs=in_specs, out_specs=out_specs, check_vma=False)
```

```python
import functools
import math

import jax
import jax.numpy as jnp
from jax import lax
from jax.experimental import pallas as pl
from jax.experimental.pallas import tpu as pltpu
from jax.sharding import PartitionSpec as P

HBM = pl.BlockSpec(memory_space=pl.ANY)
VMEM = pl.BlockSpec(memory_space=pltpu.VMEM)
SMEM = pl.BlockSpec(memory_space=pltpu.SMEM)
TILE = 256


def fetch_kernel(slots_ref, pool_ref, send_ref, sems):
    groups, levels = send_ref.shape[:2]
    me = lax.axis_index("pool")
    copies = []
    for dest in range(groups):
        for level in range(levels):
            slot = slots_ref[dest, level, me]
            copies.append(
                pltpu.make_async_copy(
                    pool_ref.at[:, :, slot], send_ref.at[dest, level], sems.at[dest, level]
                )
            )
    for copy in copies:
        copy.start()
    for copy in copies:
        copy.wait()


def back_kernel(length_ref, start_ref, suffix_ref, send_ref, sems):
    groups = send_ref.shape[0]
    pages = suffix_ref.shape[2]
    me = lax.axis_index("pool")
    first = start_ref[me] + length_ref[me]

    def each(act):
        for dest in range(groups):
            offset = lax.rem(dest + 4 * groups - lax.rem(first, groups), groups)

            @pl.when(offset < pages)
            def _():
                act(
                    pltpu.make_async_copy(
                        suffix_ref.at[:, :, jnp.minimum(offset, pages - 1)],
                        send_ref.at[dest],
                        sems.at[dest],
                    )
                )

    each(lambda copy: copy.start())
    each(lambda copy: copy.wait())


def place_kernel(pages, length_ref, start_ref, slots_ref, back_ref, pool_ref, new_ref, sems):
    del pool_ref
    requests, levels, groups = slots_ref.shape
    me = lax.axis_index("pool")

    def each(act):
        for request in range(requests):
            length = length_ref[request]
            offset = lax.rem(me + 4 * groups - lax.rem(start_ref[request] + length, groups), groups)

            @pl.when(offset < pages)
            def _():
                level = jnp.minimum(lax.div(length + offset, groups), levels - 1)
                slot = slots_ref[request, level, me]
                act(
                    pltpu.make_async_copy(
                        back_ref.at[request], new_ref.at[:, :, slot], sems.at[request]
                    )
                )

    each(lambda copy: copy.start())
    each(lambda copy: copy.wait())


def attend_kernel(
    scale,
    per_step,
    length_ref,
    start_ref,
    query_ref,
    suffix_ref,
    page_ref,
    pool_ref,
    out_ref,
    new_ref,
    keys,
    values,
    sem,
):
    groups, levels = page_ref.shape[:2]
    page_len, head_dim = page_ref.shape[4:]
    suffix = query_ref.shape[0]
    steps = pl.num_programs(1)
    head, step = pl.program_id(0), pl.program_id(1)
    me = lax.axis_index("pool")
    copy = pltpu.make_async_copy(pool_ref, new_ref, sem)

    @pl.when((head == 0) & (step == 0))
    def _():
        copy.start()

    @pl.when(step == 0)
    def _():
        length, first = length_ref[me], start_ref[me]
        keys[pl.ds(0, suffix), :] = suffix_ref[0, 0]
        values[pl.ds(0, suffix), pl.ds(0, head_dim)] = suffix_ref[1, 0]
        values[pl.ds(0, suffix), pl.ds(head_dim, head_dim)] = jnp.ones(
            (suffix, head_dim), values.dtype
        )
        for owner in range(groups):
            for level in range(levels):
                row = suffix + (owner * levels + level) * page_len
                number = level * groups + lax.rem(owner + groups - first, groups)
                seen = number < length
                key_owner = jnp.where(seen, owner, first)
                key_level = jnp.where(seen, level, 0)
                keys[pl.ds(row, page_len), :] = page_ref[key_owner, key_level, 0, 0]

                @pl.when(seen)
                def _():
                    values[pl.ds(row, page_len), pl.ds(0, head_dim)] = page_ref[owner, level, 1, 0]
                    values[pl.ds(row, page_len), pl.ds(head_dim, head_dim)] = jnp.ones(
                        (page_len, head_dim), values.dtype
                    )

                @pl.when(jnp.logical_not(seen))
                def _():
                    values[pl.ds(row, page_len), :] = jnp.zeros(
                        (page_len, 2 * head_dim), values.dtype
                    )

    tile = min(TILE, suffix)
    total = keys.shape[0]
    seen = lax.broadcasted_iota(jnp.int32, (tile, tile), 1) <= lax.broadcasted_iota(
        jnp.int32, (tile, tile), 0
    )
    contract = (((1,), (1,)), ((), ()))
    dot = functools.partial(lax.dot_general, preferred_element_type=jnp.float32)
    plain = (((1,), (0,)), ((), ()))
    for column in range(per_step):
        lanes = pl.ds(column * head_dim, head_dim)
        for row in range(0, suffix, tile):
            query = query_ref[pl.ds(row, tile), lanes]
            parts = [
                (
                    jnp.where(
                        seen, dot(query, keys[pl.ds(row, tile), :], contract), -jnp.inf
                    ),
                    values[pl.ds(row, tile), :],
                )
            ]
            if row:
                parts.append((dot(query, keys[pl.ds(0, row), :], contract), values[pl.ds(0, row), :]))
            parts.append(
                (
                    dot(query, keys[pl.ds(suffix, total - suffix), :], contract),
                    values[pl.ds(suffix, total - suffix), :],
                )
            )
            top = functools.reduce(
                jnp.maximum, [jnp.max(score, axis=1, keepdims=True) for score, _ in parts]
            )
            mixed = None
            for score, value in parts:
                weight = jnp.exp2((score - top) * scale).astype(jnp.bfloat16)
                part = dot(weight, value, plain)
                mixed = part if mixed is None else mixed + part
            out_ref[pl.ds(row, tile), lanes] = (
                mixed[:, :head_dim] / mixed[:, head_dim:]
            ).astype(out_ref.dtype)

    @pl.when((head == pl.num_programs(0) - 1) & (step == steps - 1))
    def _():
        copy.wait()


def body(queries, suffix_kv, pool_kv, prefix_pages, owner_start, page_slot):
    _, heads, slots, page_len, head_dim = pool_kv.shape
    requests, groups, levels = page_slot.shape
    suffix = queries.shape[0]
    per_kv = queries.shape[1] // (heads * head_dim)
    pages = suffix // page_len
    fetched = -(-(levels * groups - pages) // groups)
    page = (2, heads, page_len, head_dim)
    slot_of = jnp.swapaxes(page_slot, 1, 2)
    dtype = pool_kv.dtype

    send = pl.pallas_call(
        fetch_kernel,
        out_shape=pltpu.VMEM((groups, fetched) + page, dtype),
        in_specs=[SMEM, HBM],
        out_specs=VMEM,
        scratch_shapes=[pltpu.SemaphoreType.DMA((groups, fetched))],
        name="gather_pages",
    )(slot_of, pool_kv)
    received = lax.all_to_all(send, "pool", split_axis=0, concat_axis=0, tiled=True)

    back_send = pl.pallas_call(
        back_kernel,
        out_shape=pltpu.VMEM((groups,) + page, dtype),
        in_specs=[SMEM, SMEM, HBM],
        out_specs=VMEM,
        scratch_shapes=[pltpu.SemaphoreType.DMA((groups,))],
        name="pick_suffix",
    )(prefix_pages, owner_start, suffix_kv.reshape(2, heads, pages, page_len, head_dim))
    returned = lax.all_to_all(back_send, "pool", split_axis=0, concat_axis=0, tiled=True)

    per_step = math.gcd(per_kv, 4)
    steps = per_kv // per_step
    total = suffix + fetched * groups * page_len
    result, new_pool = pl.pallas_call(
        functools.partial(attend_kernel, math.log2(math.e) / math.sqrt(head_dim), per_step),
        grid=(heads, steps),
        out_shape=(
            jax.ShapeDtypeStruct(queries.shape, dtype),
            jax.ShapeDtypeStruct(pool_kv.shape, dtype),
        ),
        in_specs=[
            SMEM,
            SMEM,
            pl.BlockSpec((suffix, per_step * head_dim), lambda h, s: (0, h * steps + s)),
            pl.BlockSpec((2, 1, suffix, head_dim), lambda h, s: (0, h, 0, 0)),
            pl.BlockSpec(
                (groups, fetched, 2, 1, page_len, head_dim), lambda h, s: (0, 0, 0, h, 0, 0)
            ),
            HBM,
        ],
        out_specs=(
            pl.BlockSpec((suffix, per_step * head_dim), lambda h, s: (0, h * steps + s)),
            HBM,
        ),
        scratch_shapes=[
            pltpu.VMEM((total, head_dim), dtype),
            pltpu.VMEM((total, 2 * head_dim), dtype),
            pltpu.SemaphoreType.DMA(()),
        ],
        compiler_params=pltpu.CompilerParams(vmem_limit_bytes=48 * 1024 * 1024),
        cost_estimate=pl.CostEstimate(
            flops=4 * heads * per_kv * suffix * total * head_dim,
            bytes_accessed=4 * queries.size + 8 * pool_kv.size,
            transcendentals=heads * per_kv * suffix * total,
        ),
        name="attend",
    )(prefix_pages, owner_start, queries, suffix_kv, received, pool_kv)

    new_pool = pl.pallas_call(
        functools.partial(place_kernel, pages),
        out_shape=jax.ShapeDtypeStruct(pool_kv.shape, dtype),
        in_specs=[SMEM, SMEM, SMEM, VMEM, HBM],
        out_specs=HBM,
        input_output_aliases={4: 0},
        scratch_shapes=[pltpu.SemaphoreType.DMA((requests,))],
        name="place_pages",
    )(prefix_pages, owner_start, slot_of, returned, new_pool)
    return (result, new_pool)


def solution(mesh):
    in_specs = (
        P(("parts", "pool"), "tp"),
        P(None, "tp", ("parts", "pool"), None),
        P(None, "tp", ("parts", "pool"), None, None),
        P("parts"),
        P("parts"),
        P("parts", None, None),
    )
    out_specs = (P(("parts", "pool"), "tp"), P(None, "tp", ("parts", "pool"), None, None))
    return jax.shard_map(body, mesh=mesh, in_specs=in_specs, out_specs=out_specs, check_vma=False)
```

```python
import functools
import math

import jax
import jax.numpy as jnp
from jax import lax
from jax.experimental import pallas as pl
from jax.experimental.pallas import tpu as pltpu
from jax.sharding import PartitionSpec as P

HBM = pl.BlockSpec(memory_space=pl.ANY)
VMEM = pl.BlockSpec(memory_space=pltpu.VMEM)
SMEM = pl.BlockSpec(memory_space=pltpu.SMEM)
TILE = 256


def partner(index, step, groups):
    if groups & (groups - 1):
        return (index + step) % groups, (index + groups - step) % groups
    return index ^ step, index ^ step


def fetch_kernel(slots_ref, pool_ref, *rest):
    sends, sems = rest[:-1], rest[-1]
    groups = slots_ref.shape[2]
    levels = sends[0].shape[0]
    me = lax.axis_index("pool")
    copies = []
    for step in range(groups - 1, 0, -1):
        dest = partner(me, step, groups)[0]
        for level in range(levels):
            slot = slots_ref[dest, level, me]
            copies.append(
                pltpu.make_async_copy(
                    pool_ref.at[:, :, slot], sends[step - 1].at[level], sems.at[step, level]
                )
            )
    for copy in copies:
        copy.start()
    for copy in copies:
        copy.wait()


def back_kernel(length_ref, start_ref, suffix_ref, *rest):
    sends, sems = rest[:-1], rest[-1]
    groups = len(sends)
    pages = suffix_ref.shape[2]
    me = lax.axis_index("pool")
    first = lax.rem(start_ref[me] + length_ref[me], groups)

    def each(act):
        for step in range(groups):
            offset = lax.rem(partner(me, step, groups)[0] + groups - first, groups)

            @pl.when(offset < pages)
            def _():
                act(
                    pltpu.make_async_copy(
                        suffix_ref.at[:, :, jnp.minimum(offset, pages - 1)],
                        sends[step],
                        sems.at[step],
                    )
                )

    each(lambda copy: copy.start())
    each(lambda copy: copy.wait())


def place_kernel(pages, length_ref, start_ref, slots_ref, *rest):
    backs, new_ref, sems = rest[:-3], rest[-2], rest[-1]
    _, levels, groups = slots_ref.shape
    me = lax.axis_index("pool")

    def each(act):
        for step in range(groups):
            request = partner(me, step, groups)[1]
            length = length_ref[request]
            first = lax.rem(start_ref[request] + length, groups)
            offset = lax.rem(me + groups - first, groups)

            @pl.when(offset < pages)
            def _():
                level = jnp.minimum(lax.div(length + offset, groups), levels - 1)
                slot = slots_ref[request, level, me]
                act(
                    pltpu.make_async_copy(backs[step], new_ref.at[:, :, slot], sems.at[step])
                )

    each(lambda copy: copy.start())
    each(lambda copy: copy.wait())


def attend_kernel(
    scale, per_step, length_ref, start_ref, slots_ref, query_ref, suffix_ref, pool_ref, *rest
):
    *page_refs, out_ref, new_ref, keys, values, sem = rest
    groups = slots_ref.shape[2]
    levels = page_refs[0].shape[0]
    page_len, head_dim = pool_ref.shape[3:]
    suffix = query_ref.shape[0]
    head, step = pl.program_id(0), pl.program_id(1)
    me = lax.axis_index("pool")
    copy = pltpu.make_async_copy(pool_ref, new_ref.at[:, pl.ds(head, 1)], sem)

    @pl.when(step == 0)
    def _():
        copy.start()
        length, first = length_ref[me], start_ref[me]
        keys[pl.ds(0, suffix), :] = suffix_ref[0, 0]
        values[pl.ds(0, suffix), pl.ds(0, head_dim)] = suffix_ref[1, 0]
        values[pl.ds(0, suffix), pl.ds(head_dim, head_dim)] = jnp.ones(
            (suffix, head_dim), values.dtype
        )
        for turn in range(groups):
            owner = partner(me, turn, groups)[1]
            for level in range(levels):
                rows = pl.ds(suffix + (turn * levels + level) * page_len, page_len)
                seen = level * groups + lax.rem(owner + groups - first, groups) < length

                @pl.when(seen)
                def _():
                    if turn:
                        keys[rows, :] = page_refs[turn - 1][level, 0, 0]
                        values[rows, pl.ds(0, head_dim)] = page_refs[turn - 1][level, 1, 0]
                    else:
                        slot = slots_ref[me, level, me]
                        keys[rows, :] = pool_ref[0, 0, slot]
                        values[rows, pl.ds(0, head_dim)] = pool_ref[1, 0, slot]
                    values[rows, pl.ds(head_dim, head_dim)] = jnp.ones(
                        (page_len, head_dim), values.dtype
                    )

                @pl.when(jnp.logical_not(seen))
                def _():
                    keys[rows, :] = jnp.broadcast_to(
                        suffix_ref[0, 0, pl.ds(0, 1), :], (page_len, head_dim)
                    )
                    values[rows, :] = jnp.zeros((page_len, 2 * head_dim), values.dtype)

    tile = min(TILE, suffix)
    total = keys.shape[0]
    seen = lax.broadcasted_iota(jnp.int32, (tile, tile), 1) <= lax.broadcasted_iota(
        jnp.int32, (tile, tile), 0
    )
    contract = (((1,), (1,)), ((), ()))
    dot = functools.partial(lax.dot_general, preferred_element_type=jnp.float32)
    plain = (((1,), (0,)), ((), ()))
    for column in range(per_step):
        lanes = pl.ds(column * head_dim, head_dim)
        for row in range(0, suffix, tile):
            query = query_ref[pl.ds(row, tile), lanes]
            parts = [
                (
                    jnp.where(
                        seen, dot(query, keys[pl.ds(row, tile), :], contract), -jnp.inf
                    ),
                    values[pl.ds(row, tile), :],
                )
            ]
            if row:
                parts.append((dot(query, keys[pl.ds(0, row), :], contract), values[pl.ds(0, row), :]))
            parts.append(
                (
                    dot(query, keys[pl.ds(suffix, total - suffix), :], contract),
                    values[pl.ds(suffix, total - suffix), :],
                )
            )
            top = functools.reduce(
                jnp.maximum, [jnp.max(score, axis=1, keepdims=True) for score, _ in parts]
            )
            mixed = None
            for score, value in parts:
                weight = jnp.exp2((score - top) * scale).astype(jnp.bfloat16)
                part = dot(weight, value, plain)
                mixed = part if mixed is None else mixed + part
            out_ref[pl.ds(row, tile), lanes] = (
                mixed[:, :head_dim] / mixed[:, head_dim:]
            ).astype(out_ref.dtype)

    @pl.when(step == pl.num_programs(1) - 1)
    def _():
        copy.wait()


def body(queries, suffix_kv, pool_kv, prefix_pages, owner_start, page_slot):
    _, heads, slots, page_len, head_dim = pool_kv.shape
    _, groups, levels = page_slot.shape
    suffix = queries.shape[0]
    per_kv = queries.shape[1] // (heads * head_dim)
    pages = suffix // page_len
    fetched = -(-(levels * groups - pages) // groups)
    page = (2, heads, page_len, head_dim)
    slot_of = jnp.swapaxes(page_slot, 1, 2)
    dtype = pool_kv.dtype

    def exchange(sends):
        arrived = [None] * (groups - 1)
        for step in range(groups - 1, 0, -1):
            pairs = [(index, partner(index, step, groups)[0]) for index in range(groups)]
            arrived[step - 1] = lax.ppermute(sends[step - 1], "pool", pairs)
        return arrived

    sends = pl.pallas_call(
        fetch_kernel,
        out_shape=[pltpu.VMEM((fetched,) + page, dtype)] * (groups - 1),
        in_specs=[SMEM, HBM],
        out_specs=[VMEM] * (groups - 1),
        scratch_shapes=[pltpu.SemaphoreType.DMA((groups, fetched))],
        name="gather_pages",
    )(slot_of, pool_kv)
    received = exchange(sends)

    own_back, *back_sends = pl.pallas_call(
        back_kernel,
        out_shape=[pltpu.VMEM(page, dtype)] * groups,
        in_specs=[SMEM, SMEM, HBM],
        out_specs=[VMEM] * groups,
        scratch_shapes=[pltpu.SemaphoreType.DMA((groups,))],
        name="pick_suffix",
    )(prefix_pages, owner_start, suffix_kv.reshape(2, heads, pages, page_len, head_dim))
    returned = exchange(back_sends)

    per_step = math.gcd(per_kv, 4)
    steps = per_kv // per_step
    total = suffix + fetched * groups * page_len
    result, new_pool = pl.pallas_call(
        functools.partial(attend_kernel, math.log2(math.e) / math.sqrt(head_dim), per_step),
        grid=(heads, steps),
        out_shape=(
            jax.ShapeDtypeStruct(queries.shape, dtype),
            jax.ShapeDtypeStruct(pool_kv.shape, dtype),
        ),
        in_specs=[
            SMEM,
            SMEM,
            SMEM,
            pl.BlockSpec((suffix, per_step * head_dim), lambda h, s: (0, h * steps + s)),
            pl.BlockSpec((2, 1, suffix, head_dim), lambda h, s: (0, h, 0, 0)),
            pl.BlockSpec((2, 1, slots, page_len, head_dim), lambda h, s: (0, h, 0, 0, 0)),
        ]
        + [pl.BlockSpec((fetched, 2, 1, page_len, head_dim), lambda h, s: (0, 0, h, 0, 0))]
        * (groups - 1),
        out_specs=(
            pl.BlockSpec((suffix, per_step * head_dim), lambda h, s: (0, h * steps + s)),
            HBM,
        ),
        scratch_shapes=[
            pltpu.VMEM((total, head_dim), dtype),
            pltpu.VMEM((total, 2 * head_dim), dtype),
            pltpu.SemaphoreType.DMA(()),
        ],
        compiler_params=pltpu.CompilerParams(vmem_limit_bytes=48 * 1024 * 1024),
        cost_estimate=pl.CostEstimate(
            flops=4 * heads * per_kv * suffix * total * head_dim,
            bytes_accessed=4 * queries.size + 8 * pool_kv.size,
            transcendentals=heads * per_kv * suffix * total,
        ),
        name="attend",
    )(prefix_pages, owner_start, slot_of, queries, suffix_kv, pool_kv, *received)

    new_pool = pl.pallas_call(
        functools.partial(place_kernel, pages),
        out_shape=jax.ShapeDtypeStruct(pool_kv.shape, dtype),
        in_specs=[SMEM, SMEM, SMEM] + [VMEM] * groups + [HBM],
        out_specs=HBM,
        input_output_aliases={3 + groups: 0},
        scratch_shapes=[pltpu.SemaphoreType.DMA((groups,))],
        name="place_pages",
    )(prefix_pages, owner_start, slot_of, own_back, *returned, new_pool)
    return (result, new_pool)


def solution(mesh):
    in_specs = (
        P(("parts", "pool"), "tp"),
        P(None, "tp", ("parts", "pool"), None),
        P(None, "tp", ("parts", "pool"), None, None),
        P("parts"),
        P("parts"),
        P("parts", None, None),
    )
    out_specs = (P(("parts", "pool"), "tp"), P(None, "tp", ("parts", "pool"), None, None))
    return jax.shard_map(body, mesh=mesh, in_specs=in_specs, out_specs=out_specs, check_vma=False)
```

```python
import functools
import math

import jax
import jax.numpy as jnp
from jax import lax
from jax.experimental import pallas as pl
from jax.experimental.pallas import tpu as pltpu
from jax.sharding import PartitionSpec as P

HBM = pl.BlockSpec(memory_space=pl.ANY)
VMEM = pl.BlockSpec(memory_space=pltpu.VMEM)
SMEM = pl.BlockSpec(memory_space=pltpu.SMEM)
TILE = 256


def partner(index, step, groups):
    if groups & (groups - 1):
        return (index + step) % groups, (index + groups - step) % groups
    return index ^ step, index ^ step


def fetch_kernel(slots_ref, pool_ref, *rest):
    sends, sems = rest[:-1], rest[-1]
    groups = slots_ref.shape[2]
    levels = sends[0].shape[0]
    me = lax.axis_index("pool")
    copies = []
    for step in range(groups - 1, -1, -1):
        dest = partner(me, step, groups)[0]
        for level in range(levels):
            slot = slots_ref[dest, level, me]
            copies.append(
                pltpu.make_async_copy(
                    pool_ref.at[:, :, slot], sends[step].at[level], sems.at[step, level]
                )
            )
    for copy in copies:
        copy.start()
    for copy in copies:
        copy.wait()


def place_kernel(pages, length_ref, start_ref, slots_ref, *rest):
    backs, new_ref, sems = rest[:-4], rest[-2], rest[-1]
    _, levels, groups = slots_ref.shape
    me = lax.axis_index("pool")

    def each(act):
        for step in range(groups):
            request = partner(me, step, groups)[1]
            length = length_ref[request]
            first = lax.rem(start_ref[request] + length, groups)
            offset = lax.rem(me + groups - first, groups)

            @pl.when(offset < pages)
            def _():
                level = jnp.minimum(lax.div(length + offset, groups), levels - 1)
                slot = slots_ref[request, level, me]
                act(
                    pltpu.make_async_copy(backs[step], new_ref.at[:, :, slot], sems.at[step])
                )

    each(lambda copy: copy.start())
    each(lambda copy: copy.wait())


dot = functools.partial(lax.dot_general, preferred_element_type=jnp.float32)
ACROSS = (((1,), (1,)), ((), ()))
ALONG = (((1,), (0,)), ((), ()))


def suffix_kernel(
    scale, per_step, length_ref, start_ref, query_ref, suffix_ref, pool_ref, _, *rest
):
    sum_ref, stat_ref, new_ref, *back_refs, values, sem = rest
    groups = len(back_refs)
    page_len, head_dim = pool_ref.shape[3:]
    suffix = query_ref.shape[0]
    pages = suffix // page_len
    head, step = pl.program_id(0), pl.program_id(1)
    copy = pltpu.make_async_copy(pool_ref, new_ref.at[:, pl.ds(head, 1)], sem)

    @pl.when(step == 0)
    def _():
        copy.start()
        values[:, pl.ds(0, head_dim)] = suffix_ref[1, 0]
        values[:, pl.ds(head_dim, head_dim)] = jnp.ones((suffix, head_dim), values.dtype)
        me = lax.axis_index("pool")
        first = lax.rem(start_ref[me] + length_ref[me], groups)
        for turn in range(groups):
            offset = lax.rem(partner(me, turn, groups)[0] + groups - first, groups)
            row = pl.multiple_of(jnp.minimum(offset, pages - 1) * page_len, page_len)
            for side in range(2):
                back_refs[turn][side, 0] = suffix_ref[side, 0, pl.ds(row, page_len), :]

    tile = min(TILE, suffix)
    seen = lax.broadcasted_iota(jnp.int32, (tile, tile), 1) <= lax.broadcasted_iota(
        jnp.int32, (tile, tile), 0
    )
    lane = lax.broadcasted_iota(jnp.int32, (tile, head_dim), 1)
    for row in range(0, suffix, tile):
        rows = pl.ds(row, tile)
        stat = jnp.zeros((tile, head_dim), jnp.float32)
        for column in range(per_step):
            lanes = pl.ds(column * head_dim, head_dim)
            query = query_ref[rows, lanes]
            score = jnp.where(seen, dot(query, suffix_ref[0, 0, rows, :], ACROSS), -jnp.inf)
            top = jnp.max(score, axis=1, keepdims=True)
            if row:
                early = dot(query, suffix_ref[0, 0, pl.ds(0, row), :], ACROSS)
                top = jnp.maximum(top, jnp.max(early, axis=1, keepdims=True))
            mixed = dot(
                jnp.exp2((score - top) * scale).astype(jnp.bfloat16), values[rows, :], ALONG
            )
            if row:
                mixed += dot(
                    jnp.exp2((early - top) * scale).astype(jnp.bfloat16),
                    values[pl.ds(0, row), :],
                    ALONG,
                )
            sum_ref[rows, lanes] = mixed[:, :head_dim]
            stat = jnp.where(lane == column, top, stat)
            stat = jnp.where(lane == per_step + column, mixed[:, head_dim:], stat)
        stat_ref[0, rows, :] = stat

    @pl.when(step == pl.num_programs(1) - 1)
    def _():
        copy.wait()


def prefix_kernel(
    scale, per_step, length_ref, start_ref, query_ref, suffix_ref, sum_ref, stat_ref, *rest
):
    *page_refs, out_ref, keys, values = rest
    groups = len(page_refs)
    levels, _, _, page_len, head_dim = page_refs[0].shape
    suffix = query_ref.shape[0]

    @pl.when(pl.program_id(1) == 0)
    def _():
        me = lax.axis_index("pool")
        length, first = length_ref[me], start_ref[me]
        for turn in range(groups):
            owner = partner(me, turn, groups)[1]
            for level in range(levels):
                rows = pl.ds((turn * levels + level) * page_len, page_len)
                seen = level * groups + lax.rem(owner + groups - first, groups) < length

                @pl.when(seen)
                def _():
                    keys[rows, :] = page_refs[turn][level, 0, 0]
                    values[rows, pl.ds(0, head_dim)] = page_refs[turn][level, 1, 0]
                    values[rows, pl.ds(head_dim, head_dim)] = jnp.ones(
                        (page_len, head_dim), values.dtype
                    )

                @pl.when(jnp.logical_not(seen))
                def _():
                    keys[rows, :] = jnp.broadcast_to(
                        suffix_ref[0, 0, pl.ds(0, 1), :], (page_len, head_dim)
                    )
                    values[rows, :] = jnp.zeros((page_len, 2 * head_dim), values.dtype)

    tile = min(TILE, suffix)
    for column in range(per_step):
        lanes = pl.ds(column * head_dim, head_dim)
        for row in range(0, suffix, tile):
            rows = pl.ds(row, tile)
            score = dot(query_ref[rows, lanes], keys[...], ACROSS)
            before = stat_ref[0, rows, pl.ds(column, 1)]
            count = stat_ref[0, rows, pl.ds(per_step + column, 1)]
            top = jnp.maximum(before, jnp.max(score, axis=1, keepdims=True))
            factor = jnp.exp2((before - top) * scale)
            weight = jnp.exp2((score - top) * scale).astype(jnp.bfloat16)
            mixed = dot(weight, values[...], ALONG)
            total = mixed[:, head_dim:] + count * factor
            out_ref[rows, lanes] = (
                (mixed[:, :head_dim] + sum_ref[rows, lanes] * factor) / total
            ).astype(out_ref.dtype)


def body(queries, suffix_kv, pool_kv, prefix_pages, owner_start, page_slot):
    _, heads, slots, page_len, head_dim = pool_kv.shape
    _, groups, levels = page_slot.shape
    suffix = queries.shape[0]
    per_kv = queries.shape[1] // (heads * head_dim)
    pages = suffix // page_len
    fetched = -(-(levels * groups - pages) // groups)
    page = (2, heads, page_len, head_dim)
    slot_of = jnp.swapaxes(page_slot, 1, 2)
    dtype = pool_kv.dtype

    def exchange(sends):
        arrived = [sends[0]] + [None] * (groups - 1)
        for step in range(groups - 1, 0, -1):
            pairs = [(index, partner(index, step, groups)[0]) for index in range(groups)]
            arrived[step] = lax.ppermute(sends[step], "pool", pairs)
        return arrived

    sends = pl.pallas_call(
        fetch_kernel,
        out_shape=[pltpu.VMEM((fetched,) + page, dtype)] * groups,
        in_specs=[SMEM, HBM],
        out_specs=[VMEM] * groups,
        scratch_shapes=[pltpu.SemaphoreType.DMA((groups, fetched))],
        name="gather_pages",
    )(slot_of, pool_kv)
    received = exchange(sends)

    per_step = math.gcd(per_kv, 4)
    steps = per_kv // per_step
    scale = math.log2(math.e) / math.sqrt(head_dim)
    total = fetched * groups * page_len
    params = pltpu.CompilerParams(vmem_limit_bytes=60 * 1024 * 1024)
    columns = pl.BlockSpec((suffix, per_step * head_dim), lambda h, s: (0, h * steps + s))
    stats = pl.BlockSpec((1, suffix, head_dim), lambda h, s: (h * steps + s, 0, 0))

    def cost(keys):
        cells = heads * per_kv * suffix * keys
        return pl.CostEstimate(
            flops=6 * cells * head_dim, bytes_accessed=8 * queries.size, transcendentals=cells
        )

    sums, counts, new_pool, *back_sends = pl.pallas_call(
        functools.partial(suffix_kernel, scale, per_step),
        grid=(heads, steps),
        out_shape=[
            jax.ShapeDtypeStruct(queries.shape, jnp.float32),
            jax.ShapeDtypeStruct((heads * steps, suffix, head_dim), jnp.float32),
            jax.ShapeDtypeStruct(pool_kv.shape, dtype),
        ]
        + [jax.ShapeDtypeStruct(page, dtype)] * groups,
        in_specs=[
            SMEM,
            SMEM,
            columns,
            pl.BlockSpec((2, 1, suffix, head_dim), lambda h, s: (0, h, 0, 0)),
            pl.BlockSpec((2, 1, slots, page_len, head_dim), lambda h, s: (0, h, 0, 0, 0)),
            HBM,
        ],
        out_specs=[columns, stats, HBM]
        + [pl.BlockSpec((2, 1, page_len, head_dim), lambda h, s: (0, h, 0, 0))] * groups,
        scratch_shapes=[
            pltpu.VMEM((suffix, 2 * head_dim), dtype),
            pltpu.SemaphoreType.DMA(()),
        ],
        compiler_params=params,
        cost_estimate=cost(suffix),
        name="attend_suffix",
    )(prefix_pages, owner_start, queries, suffix_kv, pool_kv, sends[0])
    returned = exchange(back_sends)

    result = pl.pallas_call(
        functools.partial(prefix_kernel, scale, per_step),
        grid=(heads, steps),
        out_shape=jax.ShapeDtypeStruct(queries.shape, dtype),
        in_specs=[
            SMEM,
            SMEM,
            columns,
            pl.BlockSpec((1, 1, page_len, head_dim), lambda h, s: (0, h, 0, 0)),
            columns,
            stats,
        ]
        + [pl.BlockSpec((fetched, 2, 1, page_len, head_dim), lambda h, s: (0, 0, h, 0, 0))]
        * groups,
        out_specs=columns,
        scratch_shapes=[
            pltpu.VMEM((total, head_dim), dtype),
            pltpu.VMEM((total, 2 * head_dim), dtype),
        ],
        compiler_params=params,
        cost_estimate=cost(total),
        name="attend_prefix",
    )(prefix_pages, owner_start, queries, suffix_kv, sums, counts, *received)

    new_pool = pl.pallas_call(
        functools.partial(place_kernel, pages),
        out_shape=jax.ShapeDtypeStruct(pool_kv.shape, dtype),
        in_specs=[SMEM, SMEM, SMEM] + [VMEM] * groups + [HBM, HBM],
        out_specs=HBM,
        input_output_aliases={4 + groups: 0},
        scratch_shapes=[pltpu.SemaphoreType.DMA((groups,))],
        compiler_params=params,
        name="place_pages",
    )(prefix_pages, owner_start, slot_of, *returned, result, new_pool)
    return (result, new_pool)


def solution(mesh):
    in_specs = (
        P(("parts", "pool"), "tp"),
        P(None, "tp", ("parts", "pool"), None),
        P(None, "tp", ("parts", "pool"), None, None),
        P("parts"),
        P("parts"),
        P("parts", None, None),
    )
    out_specs = (P(("parts", "pool"), "tp"), P(None, "tp", ("parts", "pool"), None, None))
    return jax.shard_map(body, mesh=mesh, in_specs=in_specs, out_specs=out_specs, check_vma=False)
```

```python
import functools
import math

import jax
import jax.numpy as jnp
from jax import lax
from jax.experimental import pallas as pl
from jax.experimental.pallas import tpu as pltpu
from jax.sharding import PartitionSpec as P

HBM = pl.BlockSpec(memory_space=pl.ANY)
VMEM = pl.BlockSpec(memory_space=pltpu.VMEM)
SMEM = pl.BlockSpec(memory_space=pltpu.SMEM)
TILE = 256
COUNTS = 16


def partner(index, step, groups):
    if groups & (groups - 1):
        return (index + step) % groups, (index + groups - step) % groups
    return index ^ step, index ^ step


def fetch_kernel(slots_ref, pool_ref, *rest):
    *sends, own_ref, sems = rest
    groups = slots_ref.shape[2]
    levels = sends[0].shape[0]
    me = lax.axis_index("pool")
    copies = []
    for step in range(groups - 1, 0, -1):
        dest = partner(me, step, groups)[0]
        for level in range(levels):
            slot = slots_ref[dest, level, me]
            copies.append(
                pltpu.make_async_copy(
                    pool_ref.at[:, :, slot], sends[step - 1].at[level], sems.at[step, level]
                )
            )
    for copy in copies:
        copy.start()
    for level in range(levels):
        own_ref[level] = slots_ref[me, level, me]
    for copy in copies:
        copy.wait()


def place_kernel(pages, length_ref, start_ref, slots_ref, *rest):
    backs, new_ref, sems = rest[:-4], rest[-2], rest[-1]
    _, levels, groups = slots_ref.shape
    me = lax.axis_index("pool")

    def each(act):
        for step in range(groups):
            request = partner(me, step, groups)[1]
            length = length_ref[request]
            first = lax.rem(start_ref[request] + length, groups)
            offset = lax.rem(me + groups - first, groups)

            @pl.when(offset < pages)
            def _():
                level = jnp.minimum(lax.div(length + offset, groups), levels - 1)
                slot = slots_ref[request, level, me]
                act(
                    pltpu.make_async_copy(backs[step], new_ref.at[:, :, slot], sems.at[step])
                )

    each(lambda copy: copy.start())
    each(lambda copy: copy.wait())


dot = functools.partial(lax.dot_general, preferred_element_type=jnp.float32)
ACROSS = (((1,), (1,)), ((), ()))
ALONG = (((1,), (0,)), ((), ()))


def spread(values, rows, page):
    head_dim = page.shape[1]
    values[pl.ds(0, head_dim), rows] = page.astype(jnp.float32).T.astype(values.dtype)
    values[pl.ds(head_dim, COUNTS), rows] = jnp.ones((COUNTS, page.shape[0]), values.dtype)


def suffix_kernel(
    scale, per_step, length_ref, start_ref, own_ref, query_ref, suffix_ref, pool_ref, *rest
):
    sum_ref, stat_ref, new_ref, page_ref, *back_refs, values, sem = rest
    groups = len(back_refs)
    page_len, head_dim = pool_ref.shape[3:]
    suffix = query_ref.shape[0]
    pages = suffix // page_len
    head, step = pl.program_id(0), pl.program_id(1)
    copy = pltpu.make_async_copy(pool_ref, new_ref.at[:, pl.ds(head, 1)], sem)

    @pl.when(step == 0)
    def _():
        copy.start()
        spread(values, pl.ds(0, suffix), suffix_ref[1, 0])
        me = lax.axis_index("pool")
        first = lax.rem(start_ref[me] + length_ref[me], groups)
        for turn in range(groups):
            offset = lax.rem(partner(me, turn, groups)[0] + groups - first, groups)
            row = pl.multiple_of(jnp.minimum(offset, pages - 1) * page_len, page_len)
            for side in range(2):
                back_refs[turn][side, 0] = suffix_ref[side, 0, pl.ds(row, page_len), :]
        for level in range(page_ref.shape[0]):
            for side in range(2):
                page_ref[level, side, 0] = pool_ref[side, 0, own_ref[level]]

    tile = min(TILE, suffix)
    seen = lax.broadcasted_iota(jnp.int32, (tile, tile), 0) <= lax.broadcasted_iota(
        jnp.int32, (tile, tile), 1
    )
    for column in range(per_step):
        lanes = pl.ds(column * head_dim, head_dim)
        for row in range(0, suffix, tile):
            rows = pl.ds(row, tile)
            query = query_ref[rows, lanes]
            score = jnp.where(seen, dot(suffix_ref[0, 0, rows, :], query, ACROSS), -jnp.inf)
            top = jnp.max(score, axis=0, keepdims=True)
            if row:
                early = dot(suffix_ref[0, 0, pl.ds(0, row), :], query, ACROSS)
                top = jnp.maximum(top, jnp.max(early, axis=0, keepdims=True))
            mixed = dot(
                values[:, rows], jnp.exp2((score - top) * scale).astype(jnp.bfloat16), ALONG
            )
            if row:
                mixed += dot(
                    values[:, pl.ds(0, row)],
                    jnp.exp2((early - top) * scale).astype(jnp.bfloat16),
                    ALONG,
                )
            sum_ref[lanes, rows] = mixed[:head_dim]
            stat_ref[0, pl.ds(column, 1), rows] = top
            stat_ref[0, pl.ds(per_step + column, 1), rows] = mixed[head_dim : head_dim + 1]

    @pl.when(step == pl.num_programs(1) - 1)
    def _():
        copy.wait()


def prefix_kernel(
    scale, per_step, length_ref, start_ref, query_ref, suffix_ref, sum_ref, stat_ref, *rest
):
    *page_refs, out_ref, keys, values = rest
    groups = len(page_refs)
    levels, _, _, page_len, head_dim = page_refs[0].shape
    suffix = query_ref.shape[0]

    @pl.when(pl.program_id(1) == 0)
    def _():
        me = lax.axis_index("pool")
        length, first = length_ref[me], start_ref[me]
        for turn in range(groups):
            owner = partner(me, turn, groups)[1]
            for level in range(levels):
                rows = pl.ds((turn * levels + level) * page_len, page_len)
                seen = level * groups + lax.rem(owner + groups - first, groups) < length

                @pl.when(seen)
                def _():
                    keys[rows, :] = page_refs[turn][level, 0, 0]
                    spread(values, rows, page_refs[turn][level, 1, 0])

                @pl.when(jnp.logical_not(seen))
                def _():
                    keys[rows, :] = jnp.broadcast_to(
                        suffix_ref[0, 0, pl.ds(0, 1), :], (page_len, head_dim)
                    )
                    values[:, rows] = jnp.zeros((values.shape[0], page_len), values.dtype)

    tile = min(TILE, suffix)
    for column in range(per_step):
        lanes = pl.ds(column * head_dim, head_dim)
        for row in range(0, suffix, tile):
            rows = pl.ds(row, tile)
            score = dot(keys[...], query_ref[rows, lanes], ACROSS)
            before = stat_ref[0, pl.ds(column, 1), rows]
            count = stat_ref[0, pl.ds(per_step + column, 1), rows]
            top = jnp.maximum(before, jnp.max(score, axis=0, keepdims=True))
            factor = jnp.exp2((before - top) * scale)
            weight = jnp.exp2((score - top) * scale).astype(jnp.bfloat16)
            mixed = dot(values[...], weight, ALONG)
            share = 1.0 / (mixed[head_dim : head_dim + 1] + count * factor)
            result = mixed[:head_dim] * share + sum_ref[lanes, rows] * (factor * share)
            out_ref[rows, lanes] = result.T.astype(out_ref.dtype)


def body(queries, suffix_kv, pool_kv, prefix_pages, owner_start, page_slot):
    _, heads, slots, page_len, head_dim = pool_kv.shape
    _, groups, levels = page_slot.shape
    suffix = queries.shape[0]
    per_kv = queries.shape[1] // (heads * head_dim)
    pages = suffix // page_len
    fetched = -(-(levels * groups - pages) // groups)
    page = (2, heads, page_len, head_dim)
    slot_of = jnp.swapaxes(page_slot, 1, 2)
    dtype = pool_kv.dtype

    def exchange(sends):
        arrived = [None] * (groups - 1)
        for step in range(groups - 1, 0, -1):
            pairs = [(index, partner(index, step, groups)[0]) for index in range(groups)]
            arrived[step - 1] = lax.ppermute(sends[step - 1], "pool", pairs)
        return arrived

    *sends, own_slots = pl.pallas_call(
        fetch_kernel,
        out_shape=[pltpu.VMEM((fetched,) + page, dtype)] * (groups - 1)
        + [jax.ShapeDtypeStruct((fetched,), jnp.int32)],
        in_specs=[SMEM, HBM],
        out_specs=[VMEM] * (groups - 1) + [SMEM],
        scratch_shapes=[pltpu.SemaphoreType.DMA((groups, fetched))],
        name="gather_pages",
    )(slot_of, pool_kv)
    received = exchange(sends)

    per_step = math.gcd(per_kv, 4)
    steps = per_kv // per_step
    scale = math.log2(math.e) / math.sqrt(head_dim)
    total = fetched * groups * page_len
    params = pltpu.CompilerParams(vmem_limit_bytes=60 * 1024 * 1024)
    columns = pl.BlockSpec((suffix, per_step * head_dim), lambda h, s: (0, h * steps + s))
    turned = pl.BlockSpec((per_step * head_dim, suffix), lambda h, s: (h * steps + s, 0))
    stats = pl.BlockSpec((1, 2 * per_step, suffix), lambda h, s: (h * steps + s, 0, 0))
    pages_of = pl.BlockSpec((fetched, 2, 1, page_len, head_dim), lambda h, s: (0, 0, h, 0, 0))

    def cost(keys):
        cells = heads * per_kv * suffix * keys
        return pl.CostEstimate(
            flops=6 * cells * head_dim, bytes_accessed=8 * queries.size, transcendentals=cells
        )

    sums, counts, new_pool, own_pages, own_back, *back_sends = pl.pallas_call(
        functools.partial(suffix_kernel, scale, per_step),
        grid=(heads, steps),
        out_shape=[
            jax.ShapeDtypeStruct(queries.shape[::-1], jnp.float32),
            jax.ShapeDtypeStruct((heads * steps, 2 * per_step, suffix), jnp.float32),
            jax.ShapeDtypeStruct(pool_kv.shape, dtype),
            jax.ShapeDtypeStruct((fetched,) + page, dtype),
        ]
        + [jax.ShapeDtypeStruct(page, dtype)] * groups,
        in_specs=[
            SMEM,
            SMEM,
            SMEM,
            columns,
            pl.BlockSpec((2, 1, suffix, head_dim), lambda h, s: (0, h, 0, 0)),
            pl.BlockSpec((2, 1, slots, page_len, head_dim), lambda h, s: (0, h, 0, 0, 0)),
        ],
        out_specs=[turned, stats, HBM, pages_of]
        + [pl.BlockSpec((2, 1, page_len, head_dim), lambda h, s: (0, h, 0, 0))] * groups,
        scratch_shapes=[
            pltpu.VMEM((head_dim + COUNTS, suffix), dtype),
            pltpu.SemaphoreType.DMA(()),
        ],
        compiler_params=params,
        cost_estimate=cost(suffix),
        name="attend_suffix",
    )(prefix_pages, owner_start, own_slots, queries, suffix_kv, pool_kv)
    returned = exchange(back_sends)

    result = pl.pallas_call(
        functools.partial(prefix_kernel, scale, per_step),
        grid=(heads, steps),
        out_shape=jax.ShapeDtypeStruct(queries.shape, dtype),
        in_specs=[
            SMEM,
            SMEM,
            columns,
            pl.BlockSpec((1, 1, page_len, head_dim), lambda h, s: (0, h, 0, 0)),
            turned,
            stats,
        ]
        + [pages_of] * groups,
        out_specs=columns,
        scratch_shapes=[
            pltpu.VMEM((total, head_dim), dtype),
            pltpu.VMEM((head_dim + COUNTS, total), dtype),
        ],
        compiler_params=params,
        cost_estimate=cost(total),
        name="attend_prefix",
    )(prefix_pages, owner_start, queries, suffix_kv, sums, counts, own_pages, *received)

    new_pool = pl.pallas_call(
        functools.partial(place_kernel, pages),
        out_shape=jax.ShapeDtypeStruct(pool_kv.shape, dtype),
        in_specs=[SMEM, SMEM, SMEM] + [VMEM] * groups + [HBM, HBM],
        out_specs=HBM,
        input_output_aliases={4 + groups: 0},
        scratch_shapes=[pltpu.SemaphoreType.DMA((groups,))],
        compiler_params=params,
        name="place_pages",
    )(prefix_pages, owner_start, slot_of, own_back, *returned, result, new_pool)
    return (result, new_pool)


def solution(mesh):
    in_specs = (
        P(("parts", "pool"), "tp"),
        P(None, "tp", ("parts", "pool"), None),
        P(None, "tp", ("parts", "pool"), None, None),
        P("parts"),
        P("parts"),
        P("parts", None, None),
    )
    out_specs = (P(("parts", "pool"), "tp"), P(None, "tp", ("parts", "pool"), None, None))
    return jax.shard_map(body, mesh=mesh, in_specs=in_specs, out_specs=out_specs, check_vma=False)
```

```python
import functools
import math

import jax
import jax.numpy as jnp
from jax import lax
from jax.experimental import pallas as pl
from jax.experimental.pallas import tpu as pltpu
from jax.sharding import PartitionSpec as P

HBM = pl.BlockSpec(memory_space=pl.ANY)
VMEM = pl.BlockSpec(memory_space=pltpu.VMEM)
SMEM = pl.BlockSpec(memory_space=pltpu.SMEM)
TILE = 256


def partner(index, step, groups):
    if groups & (groups - 1):
        return (index + step) % groups, (index + groups - step) % groups
    return index ^ step, index ^ step


def fetch_kernel(slots_ref, pool_ref, *rest):
    *sends, own_ref, sems = rest
    groups = slots_ref.shape[2]
    levels = sends[0].shape[0]
    me = lax.axis_index("pool")
    copies = []
    for step in range(groups - 1, 0, -1):
        dest = partner(me, step, groups)[0]
        for level in range(levels):
            slot = slots_ref[dest, level, me]
            copies.append(
                pltpu.make_async_copy(
                    pool_ref.at[:, :, slot], sends[step - 1].at[level], sems.at[step, level]
                )
            )
    for copy in copies:
        copy.start()
    for level in range(levels):
        own_ref[level] = slots_ref[me, level, me]
    for copy in copies:
        copy.wait()


def place_kernel(pages, length_ref, start_ref, slots_ref, *rest):
    backs, new_ref, sems = rest[:-4], rest[-2], rest[-1]
    _, levels, groups = slots_ref.shape
    me = lax.axis_index("pool")

    def each(act):
        for step in range(groups):
            request = partner(me, step, groups)[1]
            length = length_ref[request]
            first = lax.rem(start_ref[request] + length, groups)
            offset = lax.rem(me + groups - first, groups)

            @pl.when(offset < pages)
            def _():
                level = jnp.minimum(lax.div(length + offset, groups), levels - 1)
                slot = slots_ref[request, level, me]
                act(
                    pltpu.make_async_copy(backs[step], new_ref.at[:, :, slot], sems.at[step])
                )

    each(lambda copy: copy.start())
    each(lambda copy: copy.wait())


dot = functools.partial(lax.dot_general, preferred_element_type=jnp.float32)
ACROSS = (((1,), (1,)), ((), ()))
ALONG = (((1,), (0,)), ((), ()))


def staggered(items, scores_of, finish):
    ahead = scores_of(items[0])
    for place, item in enumerate(items):
        scores = ahead
        if place + 1 < len(items):
            ahead = scores_of(items[place + 1])
        finish(item, scores)


def suffix_kernel(
    scale, per_step, length_ref, start_ref, own_ref, query_ref, suffix_ref, pool_ref, *rest
):
    sum_ref, top_ref, new_ref, page_ref, *back_refs, values, sem = rest
    groups = len(back_refs)
    page_len, head_dim = pool_ref.shape[3:]
    suffix = query_ref.shape[0]
    pages = suffix // page_len
    head, step = pl.program_id(0), pl.program_id(1)
    copy = pltpu.make_async_copy(pool_ref, new_ref.at[:, pl.ds(head, 1)], sem)

    @pl.when(step == 0)
    def _():
        copy.start()
        values[:, pl.ds(0, head_dim)] = suffix_ref[1, 0]
        values[:, pl.ds(head_dim, head_dim)] = jnp.ones((suffix, head_dim), values.dtype)
        me = lax.axis_index("pool")
        first = lax.rem(start_ref[me] + length_ref[me], groups)
        for turn in range(groups):
            offset = lax.rem(partner(me, turn, groups)[0] + groups - first, groups)
            row = pl.multiple_of(jnp.minimum(offset, pages - 1) * page_len, page_len)
            for side in range(2):
                back_refs[turn][side, 0] = suffix_ref[side, 0, pl.ds(row, page_len), :]
        for level in range(page_ref.shape[0]):
            for side in range(2):
                page_ref[level, side, 0] = pool_ref[side, 0, own_ref[level]]

    tile = min(TILE, suffix)
    seen = lax.broadcasted_iota(jnp.int32, (tile, tile), 1) <= lax.broadcasted_iota(
        jnp.int32, (tile, tile), 0
    )

    def scores_of(item):
        column, row = item
        query = query_ref[pl.ds(row, tile), pl.ds(column * head_dim, head_dim)]
        score = dot(query, suffix_ref[0, 0, pl.ds(row, tile), :], ACROSS)
        parts = [(jnp.where(seen, score, -jnp.inf), pl.ds(row, tile))]
        if row:
            early = pl.ds(0, row)
            parts.append((dot(query, suffix_ref[0, 0, early, :], ACROSS), early))
        return parts

    def finish(item, parts):
        column, row = item
        top = functools.reduce(
            jnp.maximum, [jnp.max(score, axis=1, keepdims=True) for score, _ in parts]
        )
        mixed = functools.reduce(
            jnp.add,
            [
                dot(jnp.exp2((score - top) * scale).astype(jnp.bfloat16), values[keys, :], ALONG)
                for score, keys in parts
            ],
        )
        rows = pl.ds(row, tile)
        sum_ref[rows, pl.ds(column * 2 * head_dim, 2 * head_dim)] = mixed
        top_ref[rows, pl.ds(column * head_dim, head_dim)] = jnp.broadcast_to(
            top, (tile, head_dim)
        )

    staggered(
        [(column, row) for column in range(per_step) for row in range(0, suffix, tile)],
        scores_of,
        finish,
    )

    @pl.when(step == pl.num_programs(1) - 1)
    def _():
        copy.wait()


def prefix_kernel(
    scale, per_step, length_ref, start_ref, query_ref, suffix_ref, sum_ref, top_ref, *rest
):
    *page_refs, out_ref, keys, values = rest
    groups = len(page_refs)
    levels, _, _, page_len, head_dim = page_refs[0].shape
    suffix = query_ref.shape[0]

    @pl.when(pl.program_id(1) == 0)
    def _():
        me = lax.axis_index("pool")
        length, first = length_ref[me], start_ref[me]
        for turn in range(groups):
            owner = partner(me, turn, groups)[1]
            for level in range(levels):
                rows = pl.ds((turn * levels + level) * page_len, page_len)
                seen = level * groups + lax.rem(owner + groups - first, groups) < length

                @pl.when(seen)
                def _():
                    keys[rows, :] = page_refs[turn][level, 0, 0]
                    values[rows, pl.ds(0, head_dim)] = page_refs[turn][level, 1, 0]
                    values[rows, pl.ds(head_dim, head_dim)] = jnp.ones(
                        (page_len, head_dim), values.dtype
                    )

                @pl.when(jnp.logical_not(seen))
                def _():
                    keys[rows, :] = jnp.broadcast_to(
                        suffix_ref[0, 0, pl.ds(0, 1), :], (page_len, head_dim)
                    )
                    values[rows, :] = jnp.zeros((page_len, 2 * head_dim), values.dtype)

    tile = min(TILE, suffix)

    def scores_of(item):
        column, row = item
        query = query_ref[pl.ds(row, tile), pl.ds(column * head_dim, head_dim)]
        return dot(query, keys[...], ACROSS)

    def finish(item, score):
        column, row = item
        rows = pl.ds(row, tile)
        lanes = pl.ds(column * head_dim, head_dim)
        before = top_ref[rows, lanes]
        top = jnp.maximum(before, jnp.max(score, axis=1, keepdims=True))
        factor = jnp.exp2((before - top) * scale)
        weight = jnp.concatenate(
            [
                jnp.exp2((score[:, start : start + head_dim] - top) * scale).astype(jnp.bfloat16)
                for start in range(0, score.shape[1], head_dim)
            ],
            axis=1,
        )
        mixed = dot(weight, values[...], ALONG)
        sums = sum_ref[rows, pl.ds(column * 2 * head_dim, head_dim)]
        count = sum_ref[rows, pl.ds(column * 2 * head_dim + head_dim, head_dim)]
        total = mixed[:, head_dim:] + count * factor
        out_ref[rows, lanes] = ((mixed[:, :head_dim] + sums * factor) / total).astype(
            out_ref.dtype
        )

    staggered(
        [(column, row) for column in range(per_step) for row in range(0, suffix, tile)],
        scores_of,
        finish,
    )


def body(queries, suffix_kv, pool_kv, prefix_pages, owner_start, page_slot):
    _, heads, slots, page_len, head_dim = pool_kv.shape
    _, groups, levels = page_slot.shape
    suffix = queries.shape[0]
    per_kv = queries.shape[1] // (heads * head_dim)
    pages = suffix // page_len
    fetched = -(-(levels * groups - pages) // groups)
    page = (2, heads, page_len, head_dim)
    slot_of = jnp.swapaxes(page_slot, 1, 2)
    dtype = pool_kv.dtype

    def exchange(sends):
        arrived = [None] * (groups - 1)
        for step in range(groups - 1, 0, -1):
            pairs = [(index, partner(index, step, groups)[0]) for index in range(groups)]
            arrived[step - 1] = lax.ppermute(sends[step - 1], "pool", pairs)
        return arrived

    *sends, own_slots = pl.pallas_call(
        fetch_kernel,
        out_shape=[pltpu.VMEM((fetched,) + page, dtype)] * (groups - 1)
        + [jax.ShapeDtypeStruct((fetched,), jnp.int32)],
        in_specs=[SMEM, HBM],
        out_specs=[VMEM] * (groups - 1) + [SMEM],
        scratch_shapes=[pltpu.SemaphoreType.DMA((groups, fetched))],
        name="gather_pages",
    )(slot_of, pool_kv)
    received = exchange(sends)

    per_step = math.gcd(per_kv, 4)
    steps = per_kv // per_step
    scale = math.log2(math.e) / math.sqrt(head_dim)
    total = fetched * groups * page_len
    params = pltpu.CompilerParams(vmem_limit_bytes=60 * 1024 * 1024)
    columns = pl.BlockSpec((suffix, per_step * head_dim), lambda h, s: (0, h * steps + s))
    doubled = pl.BlockSpec((suffix, 2 * per_step * head_dim), lambda h, s: (0, h * steps + s))
    pages_of = pl.BlockSpec((fetched, 2, 1, page_len, head_dim), lambda h, s: (0, 0, h, 0, 0))

    def cost(keys):
        cells = heads * per_kv * suffix * keys
        return pl.CostEstimate(
            flops=6 * cells * head_dim, bytes_accessed=8 * queries.size, transcendentals=cells
        )

    sums, tops, new_pool, own_pages, own_back, *back_sends = pl.pallas_call(
        functools.partial(suffix_kernel, scale, per_step),
        grid=(heads, steps),
        out_shape=[
            jax.ShapeDtypeStruct((suffix, 2 * queries.shape[1]), jnp.float32),
            jax.ShapeDtypeStruct(queries.shape, jnp.float32),
            jax.ShapeDtypeStruct(pool_kv.shape, dtype),
            jax.ShapeDtypeStruct((fetched,) + page, dtype),
        ]
        + [jax.ShapeDtypeStruct(page, dtype)] * groups,
        in_specs=[
            SMEM,
            SMEM,
            SMEM,
            columns,
            pl.BlockSpec((2, 1, suffix, head_dim), lambda h, s: (0, h, 0, 0)),
            pl.BlockSpec((2, 1, slots, page_len, head_dim), lambda h, s: (0, h, 0, 0, 0)),
        ],
        out_specs=[doubled, columns, HBM, pages_of]
        + [pl.BlockSpec((2, 1, page_len, head_dim), lambda h, s: (0, h, 0, 0))] * groups,
        scratch_shapes=[
            pltpu.VMEM((suffix, 2 * head_dim), dtype),
            pltpu.SemaphoreType.DMA(()),
        ],
        compiler_params=params,
        cost_estimate=cost(suffix),
        name="attend_suffix",
    )(prefix_pages, owner_start, own_slots, queries, suffix_kv, pool_kv)
    returned = exchange(back_sends)

    result = pl.pallas_call(
        functools.partial(prefix_kernel, scale, per_step),
        grid=(heads, steps),
        out_shape=jax.ShapeDtypeStruct(queries.shape, dtype),
        in_specs=[
            SMEM,
            SMEM,
            columns,
            pl.BlockSpec((1, 1, page_len, head_dim), lambda h, s: (0, h, 0, 0)),
            doubled,
            columns,
        ]
        + [pages_of] * groups,
        out_specs=columns,
        scratch_shapes=[
            pltpu.VMEM((total, head_dim), dtype),
            pltpu.VMEM((total, 2 * head_dim), dtype),
        ],
        compiler_params=params,
        cost_estimate=cost(total),
        name="attend_prefix",
    )(prefix_pages, owner_start, queries, suffix_kv, sums, tops, own_pages, *received)

    new_pool = pl.pallas_call(
        functools.partial(place_kernel, pages),
        out_shape=jax.ShapeDtypeStruct(pool_kv.shape, dtype),
        in_specs=[SMEM, SMEM, SMEM] + [VMEM] * groups + [HBM, HBM],
        out_specs=HBM,
        input_output_aliases={4 + groups: 0},
        scratch_shapes=[pltpu.SemaphoreType.DMA((groups,))],
        compiler_params=params,
        name="place_pages",
    )(prefix_pages, owner_start, slot_of, own_back, *returned, result, new_pool)
    return (result, new_pool)


def solution(mesh):
    in_specs = (
        P(("parts", "pool"), "tp"),
        P(None, "tp", ("parts", "pool"), None),
        P(None, "tp", ("parts", "pool"), None, None),
        P("parts"),
        P("parts"),
        P("parts", None, None),
    )
    out_specs = (P(("parts", "pool"), "tp"), P(None, "tp", ("parts", "pool"), None, None))
    return jax.shard_map(body, mesh=mesh, in_specs=in_specs, out_specs=out_specs, check_vma=False)
```

```python
import functools
import math

import jax
import jax.numpy as jnp
from jax import lax
from jax.experimental import pallas as pl
from jax.experimental.pallas import tpu as pltpu
from jax.sharding import PartitionSpec as P

HBM = pl.BlockSpec(memory_space=pl.ANY)
VMEM = pl.BlockSpec(memory_space=pltpu.VMEM)
SMEM = pl.BlockSpec(memory_space=pltpu.SMEM)
TILE = 256
FIRST = 16


def partner(index, step, groups):
    if groups & (groups - 1):
        return (index + step) % groups, (index + groups - step) % groups
    return index ^ step, index ^ step


def fetch_kernel(slots_ref, pool_ref, *rest):
    *sends, own_ref, sems = rest
    groups = slots_ref.shape[2]
    levels = sends[0].shape[0]
    me = lax.axis_index("pool")
    copies = []
    for step in range(groups - 1, 0, -1):
        dest = partner(me, step, groups)[0]
        for level in range(levels):
            slot = slots_ref[dest, level, me]
            copies.append(
                pltpu.make_async_copy(
                    pool_ref.at[:, :, slot], sends[step - 1].at[level], sems.at[step, level]
                )
            )
    for copy in copies:
        copy.start()
    for level in range(levels):
        own_ref[level] = slots_ref[me, level, me]
    for copy in copies:
        copy.wait()


def place_kernel(pages, length_ref, start_ref, slots_ref, *rest):
    backs, new_ref, sems = rest[:-4], rest[-2], rest[-1]
    _, levels, groups = slots_ref.shape
    me = lax.axis_index("pool")

    def each(act):
        for step in range(groups):
            request = partner(me, step, groups)[1]
            length = length_ref[request]
            first = lax.rem(start_ref[request] + length, groups)
            offset = lax.rem(me + groups - first, groups)

            @pl.when(offset < pages)
            def _():
                level = jnp.minimum(lax.div(length + offset, groups), levels - 1)
                slot = slots_ref[request, level, me]
                act(
                    pltpu.make_async_copy(backs[step], new_ref.at[:, :, slot], sems.at[step])
                )

    each(lambda copy: copy.start())
    each(lambda copy: copy.wait())


dot = functools.partial(lax.dot_general, preferred_element_type=jnp.float32)
ACROSS = (((1,), (1,)), ((), ()))
ALONG = (((1,), (0,)), ((), ()))


def staggered(items, scores_of, finish):
    ahead = scores_of(items[0])
    for place, item in enumerate(items):
        scores = ahead
        if place + 1 < len(items):
            ahead = scores_of(items[place + 1])
        finish(item, scores)


def suffix_kernel(
    scale, per_step, length_ref, start_ref, own_ref, query_ref, suffix_ref, pool_ref, *rest
):
    sum_ref, stat_ref, new_ref, key_ref, page_ref, *back_refs, values, sem = rest
    groups = len(back_refs)
    page_len, head_dim = pool_ref.shape[3:]
    suffix = query_ref.shape[0]
    pages = suffix // page_len
    head, step = pl.program_id(0), pl.program_id(1)
    copy = pltpu.make_async_copy(pool_ref, new_ref.at[:, pl.ds(head, 1)], sem)

    @pl.when(step == 0)
    def _():
        copy.start()
        key_ref[0] = suffix_ref[0, 0, pl.ds(0, FIRST), :]
        values[:, pl.ds(0, head_dim)] = suffix_ref[1, 0]
        values[:, pl.ds(head_dim, head_dim)] = jnp.ones((suffix, head_dim), values.dtype)
        me = lax.axis_index("pool")
        first = lax.rem(start_ref[me] + length_ref[me], groups)
        for turn in range(groups):
            offset = lax.rem(partner(me, turn, groups)[0] + groups - first, groups)
            row = pl.multiple_of(jnp.minimum(offset, pages - 1) * page_len, page_len)
            for side in range(2):
                back_refs[turn][side, 0] = suffix_ref[side, 0, pl.ds(row, page_len), :]
        for level in range(page_ref.shape[0]):
            for side in range(2):
                page_ref[level, side, 0] = pool_ref[side, 0, own_ref[level]]

    tile = min(TILE, suffix)
    seen = lax.broadcasted_iota(jnp.int32, (tile, tile), 1) <= lax.broadcasted_iota(
        jnp.int32, (tile, tile), 0
    )
    lane = lax.broadcasted_iota(jnp.int32, (tile, head_dim), 1)

    def scores_of(item):
        column, row = item
        query = query_ref[pl.ds(row, tile), pl.ds(column * head_dim, head_dim)]
        score = dot(query, suffix_ref[0, 0, pl.ds(row, tile), :], ACROSS)
        parts = [(jnp.where(seen, score, -jnp.inf), pl.ds(row, tile))]
        if row:
            early = pl.ds(0, row)
            parts.append((dot(query, suffix_ref[0, 0, early, :], ACROSS), early))
        return parts

    def finish(item, parts):
        column, row = item
        top = functools.reduce(
            jnp.maximum, [jnp.max(score, axis=1, keepdims=True) for score, _ in parts]
        )
        mixed = functools.reduce(
            jnp.add,
            [
                dot(jnp.exp2((score - top) * scale).astype(jnp.bfloat16), values[keys, :], ALONG)
                for score, keys in parts
            ],
        )
        rows = pl.ds(row, tile)
        sum_ref[rows, pl.ds(column * head_dim, head_dim)] = mixed[:, :head_dim]
        stat = jnp.where(lane == column, top, stat_ref[0, rows, :])
        stat_ref[0, rows, :] = jnp.where(lane == per_step + column, mixed[:, head_dim:], stat)

    staggered(
        [(column, row) for column in range(per_step) for row in range(0, suffix, tile)],
        scores_of,
        finish,
    )

    @pl.when(step == pl.num_programs(1) - 1)
    def _():
        copy.wait()


def prefix_kernel(
    scale, per_step, length_ref, start_ref, query_ref, key_ref, sum_ref, stat_ref, *rest
):
    *page_refs, out_ref, keys, values = rest
    groups = len(page_refs)
    levels, _, _, page_len, head_dim = page_refs[0].shape
    suffix = query_ref.shape[0]

    @pl.when(pl.program_id(1) == 0)
    def _():
        me = lax.axis_index("pool")
        length, first = length_ref[me], start_ref[me]
        for turn in range(groups):
            owner = partner(me, turn, groups)[1]
            for level in range(levels):
                rows = pl.ds((turn * levels + level) * page_len, page_len)
                seen = level * groups + lax.rem(owner + groups - first, groups) < length

                @pl.when(seen)
                def _():
                    keys[rows, :] = page_refs[turn][level, 0, 0]
                    values[rows, pl.ds(0, head_dim)] = page_refs[turn][level, 1, 0]
                    values[rows, pl.ds(head_dim, head_dim)] = jnp.ones(
                        (page_len, head_dim), values.dtype
                    )

                @pl.when(jnp.logical_not(seen))
                def _():
                    keys[rows, :] = jnp.broadcast_to(
                        key_ref[0, pl.ds(0, 1), :], (page_len, head_dim)
                    )
                    values[rows, :] = jnp.zeros((page_len, 2 * head_dim), values.dtype)

    tile = min(TILE, suffix)

    def scores_of(item):
        column, row = item
        query = query_ref[pl.ds(row, tile), pl.ds(column * head_dim, head_dim)]
        return dot(query, keys[...], ACROSS)

    def finish(item, score):
        column, row = item
        rows = pl.ds(row, tile)
        lanes = pl.ds(column * head_dim, head_dim)
        before, count = [
            jnp.broadcast_to(stat_ref[0, rows, pl.ds(place, 1)], (tile, head_dim))
            for place in (column, per_step + column)
        ]
        top = jnp.maximum(before, jnp.max(score, axis=1, keepdims=True))
        factor = jnp.exp2((before - top) * scale)
        weight = jnp.concatenate(
            [
                jnp.exp2((score[:, start : start + head_dim] - top) * scale).astype(jnp.bfloat16)
                for start in range(0, score.shape[1], head_dim)
            ],
            axis=1,
        )
        mixed = dot(weight, values[...], ALONG)
        total = mixed[:, head_dim:] + count * factor
        out_ref[rows, lanes] = ((mixed[:, :head_dim] + sum_ref[rows, lanes] * factor) / total).astype(
            out_ref.dtype
        )

    staggered(
        [(column, row) for column in range(per_step) for row in range(0, suffix, tile)],
        scores_of,
        finish,
    )


def body(queries, suffix_kv, pool_kv, prefix_pages, owner_start, page_slot):
    _, heads, slots, page_len, head_dim = pool_kv.shape
    _, groups, levels = page_slot.shape
    suffix = queries.shape[0]
    per_kv = queries.shape[1] // (heads * head_dim)
    pages = suffix // page_len
    fetched = -(-(levels * groups - pages) // groups)
    page = (2, heads, page_len, head_dim)
    slot_of = jnp.swapaxes(page_slot, 1, 2)
    dtype = pool_kv.dtype

    def exchange(sends):
        arrived = [None] * (groups - 1)
        for step in range(groups - 1, 0, -1):
            pairs = [(index, partner(index, step, groups)[0]) for index in range(groups)]
            arrived[step - 1] = lax.ppermute(sends[step - 1], "pool", pairs)
        return arrived

    *sends, own_slots = pl.pallas_call(
        fetch_kernel,
        out_shape=[pltpu.VMEM((fetched,) + page, dtype)] * (groups - 1)
        + [jax.ShapeDtypeStruct((fetched,), jnp.int32)],
        in_specs=[SMEM, HBM],
        out_specs=[VMEM] * (groups - 1) + [SMEM],
        scratch_shapes=[pltpu.SemaphoreType.DMA((groups, fetched))],
        name="gather_pages",
    )(slot_of, pool_kv)
    received = exchange(sends)

    per_step = math.gcd(per_kv, 4)
    steps = per_kv // per_step
    scale = math.log2(math.e) / math.sqrt(head_dim)

    def grant(size):
        return pltpu.CompilerParams(vmem_limit_bytes=size * 1024 * 1024)

    total = fetched * groups * page_len
    columns = pl.BlockSpec((suffix, per_step * head_dim), lambda h, s: (0, h * steps + s))
    stats = pl.BlockSpec((1, suffix, head_dim), lambda h, s: (h * steps + s, 0, 0))
    first_keys = pl.BlockSpec((1, FIRST, head_dim), lambda h, s: (h, 0, 0))
    pages_of = pl.BlockSpec((fetched, 2, 1, page_len, head_dim), lambda h, s: (0, 0, h, 0, 0))

    def cost(keys):
        cells = heads * per_kv * suffix * keys
        return pl.CostEstimate(
            flops=6 * cells * head_dim, bytes_accessed=8 * queries.size, transcendentals=cells
        )

    sums, counts, new_pool, keys, own_pages, own_back, *back_sends = pl.pallas_call(
        functools.partial(suffix_kernel, scale, per_step),
        grid=(heads, steps),
        out_shape=[
            jax.ShapeDtypeStruct(queries.shape, jnp.float32),
            jax.ShapeDtypeStruct((heads * steps, suffix, head_dim), jnp.float32),
            jax.ShapeDtypeStruct(pool_kv.shape, dtype),
            jax.ShapeDtypeStruct((heads, FIRST, head_dim), dtype),
            jax.ShapeDtypeStruct((fetched,) + page, dtype),
        ]
        + [jax.ShapeDtypeStruct(page, dtype)] * groups,
        in_specs=[
            SMEM,
            SMEM,
            SMEM,
            columns,
            pl.BlockSpec((2, 1, suffix, head_dim), lambda h, s: (0, h, 0, 0)),
            pl.BlockSpec((2, 1, slots, page_len, head_dim), lambda h, s: (0, h, 0, 0, 0)),
        ],
        out_specs=[columns, stats, HBM, first_keys, pages_of]
        + [pl.BlockSpec((2, 1, page_len, head_dim), lambda h, s: (0, h, 0, 0))] * groups,
        scratch_shapes=[
            pltpu.VMEM((suffix, 2 * head_dim), dtype),
            pltpu.SemaphoreType.DMA(()),
        ],
        compiler_params=grant(60),
        cost_estimate=cost(suffix),
        name="attend_suffix",
    )(prefix_pages, owner_start, own_slots, queries, suffix_kv, pool_kv)
    returned = exchange(back_sends)

    result = pl.pallas_call(
        functools.partial(prefix_kernel, scale, per_step),
        grid=(heads, steps),
        out_shape=jax.ShapeDtypeStruct(queries.shape, dtype),
        in_specs=[
            SMEM,
            SMEM,
            columns,
            first_keys,
            columns,
            stats,
        ]
        + [pages_of] * groups,
        out_specs=columns,
        scratch_shapes=[
            pltpu.VMEM((total, head_dim), dtype),
            pltpu.VMEM((total, 2 * head_dim), dtype),
        ],
        compiler_params=grant(60),
        cost_estimate=cost(total),
        name="attend_prefix",
    )(prefix_pages, owner_start, queries, keys, sums, counts, own_pages, *received)

    new_pool = pl.pallas_call(
        functools.partial(place_kernel, pages),
        out_shape=jax.ShapeDtypeStruct(pool_kv.shape, dtype),
        in_specs=[SMEM, SMEM, SMEM] + [VMEM] * groups + [HBM, HBM],
        out_specs=HBM,
        input_output_aliases={4 + groups: 0},
        scratch_shapes=[pltpu.SemaphoreType.DMA((groups,))],
        compiler_params=grant(60),
        name="place_pages",
    )(prefix_pages, owner_start, slot_of, own_back, *returned, result, new_pool)
    return (result, new_pool)


def solution(mesh):
    in_specs = (
        P(("parts", "pool"), "tp"),
        P(None, "tp", ("parts", "pool"), None),
        P(None, "tp", ("parts", "pool"), None, None),
        P("parts"),
        P("parts"),
        P("parts", None, None),
    )
    out_specs = (P(("parts", "pool"), "tp"), P(None, "tp", ("parts", "pool"), None, None))
    return jax.shard_map(body, mesh=mesh, in_specs=in_specs, out_specs=out_specs, check_vma=False)
```

```python
import functools
import math

import jax
import jax.numpy as jnp
from jax import lax
from jax.experimental import pallas as pl
from jax.experimental.pallas import tpu as pltpu
from jax.sharding import PartitionSpec as P

HBM = pl.BlockSpec(memory_space=pl.ANY)
VMEM = pl.BlockSpec(memory_space=pltpu.VMEM)
SMEM = pl.BlockSpec(memory_space=pltpu.SMEM)
TILE = 256
FIRST = 16


def partner(index, step, groups):
    if groups & (groups - 1):
        return (index + step) % groups, (index + groups - step) % groups
    return index ^ step, index ^ step


def fetch_kernel(slots_ref, pool_ref, *rest):
    *sends, own_ref, sems = rest
    groups = slots_ref.shape[2]
    levels = sends[0].shape[0]
    me = lax.axis_index("pool")
    copies = []
    for step in range(groups - 1, 0, -1):
        dest = partner(me, step, groups)[0]
        for level in range(levels):
            slot = slots_ref[dest, level, me]
            copies.append(
                pltpu.make_async_copy(
                    pool_ref.at[:, :, slot], sends[step - 1].at[level], sems.at[step, level]
                )
            )
    for copy in copies:
        copy.start()
    for level in range(levels):
        own_ref[level] = slots_ref[me, level, me]
    for copy in copies:
        copy.wait()


def place_kernel(pages, length_ref, start_ref, slots_ref, *rest):
    backs, new_ref, sems = rest[:-4], rest[-2], rest[-1]
    _, levels, groups = slots_ref.shape
    me = lax.axis_index("pool")

    def each(act):
        for step in range(groups):
            request = partner(me, step, groups)[1]
            length = length_ref[request]
            first = lax.rem(start_ref[request] + length, groups)
            offset = lax.rem(me + groups - first, groups)

            @pl.when(offset < pages)
            def _():
                level = jnp.minimum(lax.div(length + offset, groups), levels - 1)
                slot = slots_ref[request, level, me]
                act(
                    pltpu.make_async_copy(backs[step], new_ref.at[:, :, slot], sems.at[step])
                )

    each(lambda copy: copy.start())
    each(lambda copy: copy.wait())


dot = functools.partial(lax.dot_general, preferred_element_type=jnp.float32)
ACROSS = (((1,), (1,)), ((), ()))
ALONG = (((1,), (0,)), ((), ()))


def staggered(items, scores_of, finish):
    ahead = scores_of(items[0])
    for place, item in enumerate(items):
        scores = ahead
        if place + 1 < len(items):
            ahead = scores_of(items[place + 1])
        finish(item, scores)


def suffix_kernel(
    scale, per_step, length_ref, start_ref, own_ref, query_ref, suffix_ref, pool_ref, *rest
):
    mean_ref, log_ref, new_ref, key_ref, page_ref, *back_refs, values, sem = rest
    groups = len(back_refs)
    page_len, head_dim = pool_ref.shape[3:]
    suffix = query_ref.shape[0]
    pages = suffix // page_len
    head, step = pl.program_id(0), pl.program_id(1)
    copy = pltpu.make_async_copy(pool_ref, new_ref.at[:, pl.ds(head, 1)], sem)

    @pl.when(step == 0)
    def _():
        copy.start()
        key_ref[0] = suffix_ref[0, 0, pl.ds(0, FIRST), :]
        values[:, pl.ds(0, head_dim)] = suffix_ref[1, 0]
        values[:, pl.ds(head_dim, head_dim)] = jnp.ones((suffix, head_dim), values.dtype)
        me = lax.axis_index("pool")
        first = lax.rem(start_ref[me] + length_ref[me], groups)
        for turn in range(groups):
            offset = lax.rem(partner(me, turn, groups)[0] + groups - first, groups)
            row = pl.multiple_of(jnp.minimum(offset, pages - 1) * page_len, page_len)
            for side in range(2):
                back_refs[turn][side, 0] = suffix_ref[side, 0, pl.ds(row, page_len), :]
        for level in range(page_ref.shape[0]):
            for side in range(2):
                page_ref[level, side, 0] = pool_ref[side, 0, own_ref[level]]

    tile = min(TILE, suffix)
    seen = lax.broadcasted_iota(jnp.int32, (tile, tile), 1) <= lax.broadcasted_iota(
        jnp.int32, (tile, tile), 0
    )

    def scores_of(column):
        lanes = pl.ds(column * head_dim, head_dim)
        return [
            dot(query_ref[row:, lanes], suffix_ref[0, 0, pl.ds(row, tile), :], ACROSS)
            for row in range(0, suffix, tile)
        ]

    def finish(column, scores):
        lanes = pl.ds(column * head_dim, head_dim)
        scores = [
            [
                block[row : row + tile] if row else jnp.where(seen, block[:tile], -jnp.inf)
                for row in range(0, block.shape[0], tile)
            ]
            for block in scores
        ]
        blocks = len(scores)
        tops = [
            functools.reduce(
                jnp.maximum,
                [
                    jnp.max(scores[key][row - key], axis=1, keepdims=True)
                    for key in range(row + 1)
                ],
            )
            for row in range(blocks)
        ]
        mixed = [None] * blocks
        for key in range(blocks):
            weight = [
                jnp.exp2((scores[key][row - key] - tops[row]) * scale).astype(jnp.bfloat16)
                for row in range(key, blocks)
            ]
            weight = jnp.concatenate(weight, axis=0) if len(weight) > 1 else weight[0]
            part = dot(weight, values[pl.ds(key * tile, tile), :], ALONG)
            for row in range(key, blocks):
                piece = part[(row - key) * tile : (row - key + 1) * tile]
                mixed[row] = piece if mixed[row] is None else mixed[row] + piece
        for row in range(blocks):
            rows = pl.ds(row * tile, tile)
            count = mixed[row][:, head_dim:]
            mean_ref[rows, lanes] = mixed[row][:, :head_dim] / count
            log_ref[rows, lanes] = tops[row] * scale + jnp.log2(count)

    staggered(range(per_step), scores_of, finish)

    @pl.when(step == pl.num_programs(1) - 1)
    def _():
        copy.wait()


def prefix_kernel(
    scale, per_step, length_ref, start_ref, query_ref, key_ref, mean_ref, log_ref, *rest
):
    *page_refs, out_ref, keys, values = rest
    groups = len(page_refs)
    levels, _, _, page_len, head_dim = page_refs[0].shape
    suffix = query_ref.shape[0]

    @pl.when(pl.program_id(1) == 0)
    def _():
        me = lax.axis_index("pool")
        length, first = length_ref[me], start_ref[me]
        for turn in range(groups):
            owner = partner(me, turn, groups)[1]
            for level in range(levels):
                rows = pl.ds((turn * levels + level) * page_len, page_len)
                seen = level * groups + lax.rem(owner + groups - first, groups) < length

                @pl.when(seen)
                def _():
                    keys[rows, :] = page_refs[turn][level, 0, 0]
                    values[rows, pl.ds(0, head_dim)] = page_refs[turn][level, 1, 0]
                    values[rows, pl.ds(head_dim, head_dim)] = jnp.ones(
                        (page_len, head_dim), values.dtype
                    )

                @pl.when(jnp.logical_not(seen))
                def _():
                    keys[rows, :] = jnp.broadcast_to(
                        key_ref[0, pl.ds(0, 1), :], (page_len, head_dim)
                    )
                    values[rows, :] = jnp.zeros((page_len, 2 * head_dim), values.dtype)

    def scores_of(column):
        query = query_ref[:, pl.ds(column * head_dim, head_dim)]
        return dot(query, keys[...], ACROSS)

    def finish(column, score):
        lanes = pl.ds(column * head_dim, head_dim)
        before = log_ref[:, lanes]
        top = jnp.maximum(before, jnp.max(score, axis=1, keepdims=True) * scale)
        weight = jnp.concatenate(
            [
                jnp.exp2(score[:, start : start + head_dim] * scale - top).astype(jnp.bfloat16)
                for start in range(0, score.shape[1], head_dim)
            ],
            axis=1,
        )
        mixed = dot(weight, values[...], ALONG)
        share = jnp.exp2(before - top)
        out_ref[:, lanes] = (
            (mixed[:, :head_dim] + mean_ref[:, lanes] * share) / (mixed[:, head_dim:] + share)
        ).astype(out_ref.dtype)

    staggered(range(per_step), scores_of, finish)


def body(queries, suffix_kv, pool_kv, prefix_pages, owner_start, page_slot):
    _, heads, slots, page_len, head_dim = pool_kv.shape
    _, groups, levels = page_slot.shape
    suffix = queries.shape[0]
    per_kv = queries.shape[1] // (heads * head_dim)
    pages = suffix // page_len
    fetched = -(-(levels * groups - pages) // groups)
    page = (2, heads, page_len, head_dim)
    slot_of = jnp.swapaxes(page_slot, 1, 2)
    dtype = pool_kv.dtype

    def exchange(sends):
        arrived = [None] * (groups - 1)
        for step in range(groups - 1, 0, -1):
            pairs = [(index, partner(index, step, groups)[0]) for index in range(groups)]
            arrived[step - 1] = lax.ppermute(sends[step - 1], "pool", pairs)
        return arrived

    *sends, own_slots = pl.pallas_call(
        fetch_kernel,
        out_shape=[pltpu.VMEM((fetched,) + page, dtype)] * (groups - 1)
        + [jax.ShapeDtypeStruct((fetched,), jnp.int32)],
        in_specs=[SMEM, HBM],
        out_specs=[VMEM] * (groups - 1) + [SMEM],
        scratch_shapes=[pltpu.SemaphoreType.DMA((groups, fetched))],
        name="gather_pages",
    )(slot_of, pool_kv)
    received = exchange(sends)

    per_step = math.gcd(per_kv, 4)
    steps = per_kv // per_step
    scale = math.log2(math.e) / math.sqrt(head_dim)

    def grant(size):
        return pltpu.CompilerParams(vmem_limit_bytes=size * 1024 * 1024)

    total = fetched * groups * page_len
    columns = pl.BlockSpec((suffix, per_step * head_dim), lambda h, s: (0, h * steps + s))
    first_keys = pl.BlockSpec((1, FIRST, head_dim), lambda h, s: (h, 0, 0))
    pages_of = pl.BlockSpec((fetched, 2, 1, page_len, head_dim), lambda h, s: (0, 0, h, 0, 0))

    def cost(keys):
        cells = heads * per_kv * suffix * keys
        return pl.CostEstimate(
            flops=6 * cells * head_dim, bytes_accessed=8 * queries.size, transcendentals=cells
        )

    means, logs, new_pool, keys, own_pages, own_back, *back_sends = pl.pallas_call(
        functools.partial(suffix_kernel, scale, per_step),
        grid=(heads, steps),
        out_shape=[
            jax.ShapeDtypeStruct(queries.shape, jnp.float32),
            jax.ShapeDtypeStruct(queries.shape, jnp.float32),
            jax.ShapeDtypeStruct(pool_kv.shape, dtype),
            jax.ShapeDtypeStruct((heads, FIRST, head_dim), dtype),
            jax.ShapeDtypeStruct((fetched,) + page, dtype),
        ]
        + [jax.ShapeDtypeStruct(page, dtype)] * groups,
        in_specs=[
            SMEM,
            SMEM,
            SMEM,
            columns,
            pl.BlockSpec((2, 1, suffix, head_dim), lambda h, s: (0, h, 0, 0)),
            pl.BlockSpec((2, 1, slots, page_len, head_dim), lambda h, s: (0, h, 0, 0, 0)),
        ],
        out_specs=[columns, columns, HBM, first_keys, pages_of]
        + [pl.BlockSpec((2, 1, page_len, head_dim), lambda h, s: (0, h, 0, 0))] * groups,
        scratch_shapes=[
            pltpu.VMEM((suffix, 2 * head_dim), dtype),
            pltpu.SemaphoreType.DMA(()),
        ],
        compiler_params=grant(60),
        cost_estimate=cost(suffix),
        name="attend_suffix",
    )(prefix_pages, owner_start, own_slots, queries, suffix_kv, pool_kv)
    returned = exchange(back_sends)

    result = pl.pallas_call(
        functools.partial(prefix_kernel, scale, per_step),
        grid=(heads, steps),
        out_shape=jax.ShapeDtypeStruct(queries.shape, dtype),
        in_specs=[
            SMEM,
            SMEM,
            columns,
            first_keys,
            columns,
            columns,
        ]
        + [pages_of] * groups,
        out_specs=columns,
        scratch_shapes=[
            pltpu.VMEM((total, head_dim), dtype),
            pltpu.VMEM((total, 2 * head_dim), dtype),
        ],
        compiler_params=grant(60),
        cost_estimate=cost(total),
        name="attend_prefix",
    )(prefix_pages, owner_start, queries, keys, means, logs, own_pages, *received)

    new_pool = pl.pallas_call(
        functools.partial(place_kernel, pages),
        out_shape=jax.ShapeDtypeStruct(pool_kv.shape, dtype),
        in_specs=[SMEM, SMEM, SMEM] + [VMEM] * groups + [HBM, HBM],
        out_specs=HBM,
        input_output_aliases={4 + groups: 0},
        scratch_shapes=[pltpu.SemaphoreType.DMA((groups,))],
        compiler_params=grant(60),
        name="place_pages",
    )(prefix_pages, owner_start, slot_of, own_back, *returned, result, new_pool)
    return (result, new_pool)


def solution(mesh):
    in_specs = (
        P(("parts", "pool"), "tp"),
        P(None, "tp", ("parts", "pool"), None),
        P(None, "tp", ("parts", "pool"), None, None),
        P("parts"),
        P("parts"),
        P("parts", None, None),
    )
    out_specs = (P(("parts", "pool"), "tp"), P(None, "tp", ("parts", "pool"), None, None))
    return jax.shard_map(body, mesh=mesh, in_specs=in_specs, out_specs=out_specs, check_vma=False)
```

```python
import functools
import math

import jax
import jax.numpy as jnp
from jax import lax
from jax.experimental import pallas as pl
from jax.experimental.pallas import tpu as pltpu
from jax.sharding import PartitionSpec as P

HBM = pl.BlockSpec(memory_space=pl.ANY)
VMEM = pl.BlockSpec(memory_space=pltpu.VMEM)
SMEM = pl.BlockSpec(memory_space=pltpu.SMEM)
TILE = 256


def partner(index, step, groups):
    if groups & (groups - 1):
        return (index + step) % groups, (index + groups - step) % groups
    return index ^ step, index ^ step


def turn_of(index, source, groups):
    if groups & (groups - 1):
        return lax.rem(index + groups - source, groups)
    return index ^ source


def fetch_kernel(slots_ref, pool_ref, *rest):
    *sends, token_ref, sems = rest
    groups = slots_ref.shape[2]
    levels = sends[0].shape[0]
    me = lax.axis_index("pool")
    copies = []
    for step in range(groups - 1, -1, -1):
        dest = partner(me, step, groups)[0]
        for level in range(levels):
            slot = slots_ref[dest, level, me]
            copies.append(
                pltpu.make_async_copy(
                    pool_ref.at[:, :, slot], sends[step].at[level], sems.at[step, level]
                )
            )
    for copy in copies:
        copy.start()
    token_ref[0] = me
    for copy in copies:
        copy.wait()


def place_kernel(pages, length_ref, start_ref, slots_ref, *rest):
    backs, new_ref, sems = rest[:-4], rest[-2], rest[-1]
    _, levels, groups = slots_ref.shape
    me = lax.axis_index("pool")

    def each(act):
        for step in range(groups):
            request = partner(me, step, groups)[1]
            length = length_ref[request]
            first = lax.rem(start_ref[request] + length, groups)
            offset = lax.rem(me + groups - first, groups)

            @pl.when(offset < pages)
            def _():
                level = jnp.minimum(lax.div(length + offset, groups), levels - 1)
                slot = slots_ref[request, level, me]
                act(
                    pltpu.make_async_copy(backs[step], new_ref.at[:, :, slot], sems.at[step])
                )

    each(lambda copy: copy.start())
    each(lambda copy: copy.wait())


dot = functools.partial(lax.dot_general, preferred_element_type=jnp.float32)
ACROSS = (((1,), (1,)), ((), ()))
ALONG = (((1,), (0,)), ((), ()))


def staggered(items, scores_of, finish):
    ahead = scores_of(items[0])
    for place, item in enumerate(items):
        scores = ahead
        if place + 1 < len(items):
            ahead = scores_of(items[place + 1])
        finish(item, scores)


def suffix_kernel(
    scale, per_step, length_ref, start_ref, _, query_ref, suffix_ref, pool_ref, *rest
):
    mean_ref, log_ref, new_ref, *back_refs, values, sem = rest
    groups = len(back_refs)
    page_len, head_dim = pool_ref.shape[3:]
    suffix = query_ref.shape[0]
    pages = suffix // page_len
    head, step = pl.program_id(0), pl.program_id(1)
    copy = pltpu.make_async_copy(pool_ref, new_ref.at[:, pl.ds(head, 1)], sem)

    @pl.when(step == 0)
    def _():
        copy.start()
        values[:, pl.ds(0, head_dim)] = suffix_ref[1, 0]
        values[:, pl.ds(head_dim, head_dim)] = jnp.ones((suffix, head_dim), values.dtype)
        me = lax.axis_index("pool")
        first = lax.rem(start_ref[me] + length_ref[me], groups)
        for turn in range(groups):
            offset = lax.rem(partner(me, turn, groups)[0] + groups - first, groups)
            row = pl.multiple_of(jnp.minimum(offset, pages - 1) * page_len, page_len)
            for side in range(2):
                back_refs[turn][side, 0] = suffix_ref[side, 0, pl.ds(row, page_len), :]

    tile = min(TILE, suffix)
    seen = lax.broadcasted_iota(jnp.int32, (tile, tile), 1) <= lax.broadcasted_iota(
        jnp.int32, (tile, tile), 0
    )

    def scores_of(column):
        lanes = pl.ds(column * head_dim, head_dim)
        return [
            dot(query_ref[row:, lanes], suffix_ref[0, 0, pl.ds(row, tile), :], ACROSS)
            for row in range(0, suffix, tile)
        ]

    def finish(column, scores):
        lanes = pl.ds(column * head_dim, head_dim)
        scores = [
            [
                block[row : row + tile] if row else jnp.where(seen, block[:tile], -jnp.inf)
                for row in range(0, block.shape[0], tile)
            ]
            for block in scores
        ]
        blocks = len(scores)
        tops = [
            functools.reduce(
                jnp.maximum,
                [
                    jnp.max(scores[key][row - key], axis=1, keepdims=True)
                    for key in range(row + 1)
                ],
            )
            for row in range(blocks)
        ]
        mixed = [None] * blocks
        for key in range(blocks):
            weight = [
                jnp.exp2((scores[key][row - key] - tops[row]) * scale).astype(jnp.bfloat16)
                for row in range(key, blocks)
            ]
            weight = jnp.concatenate(weight, axis=0) if len(weight) > 1 else weight[0]
            part = dot(weight, values[pl.ds(key * tile, tile), :], ALONG)
            for row in range(key, blocks):
                piece = part[(row - key) * tile : (row - key + 1) * tile]
                mixed[row] = piece if mixed[row] is None else mixed[row] + piece
        for row in range(blocks):
            rows = pl.ds(row * tile, tile)
            count = mixed[row][:, head_dim:]
            mean_ref[rows, lanes] = mixed[row][:, :head_dim] / count
            log_ref[rows, lanes] = tops[row] * scale + jnp.log2(count)

    staggered(range(per_step), scores_of, finish)

    @pl.when(step == pl.num_programs(1) - 1)
    def _():
        copy.wait()


def prefix_kernel(
    scale, per_step, length_ref, start_ref, query_ref, mean_ref, log_ref, *rest
):
    *page_refs, out_ref, token_ref, keys, values = rest
    groups = len(page_refs)
    levels, _, _, page_len, head_dim = page_refs[0].shape
    suffix = query_ref.shape[0]

    token_ref[...] = jnp.zeros_like(token_ref)

    @pl.when(pl.program_id(1) == 0)
    def _():
        me = lax.axis_index("pool")
        length, first = length_ref[me], start_ref[me]
        places = []
        for turn in range(groups):
            owner = partner(me, turn, groups)[1]
            for level in range(levels):
                rows = pl.ds((turn * levels + level) * page_len, page_len)
                seen = level * groups + lax.rem(owner + groups - first, groups) < length
                places.append((rows, seen))
                keys[rows, :] = page_refs[turn][level, 0, 0]

                @pl.when(seen)
                def _():
                    values[rows, pl.ds(0, head_dim)] = page_refs[turn][level, 1, 0]
                    values[rows, pl.ds(head_dim, head_dim)] = jnp.ones(
                        (page_len, head_dim), values.dtype
                    )

        page_zero = pl.ds(
            pl.multiple_of(turn_of(me, first, groups) * levels * page_len, page_len), page_len
        )
        for rows, seen in places:

            @pl.when(jnp.logical_not(seen))
            def _():
                keys[rows, :] = keys[page_zero, :]
                values[rows, :] = jnp.zeros((page_len, 2 * head_dim), values.dtype)

    def scores_of(column):
        query = query_ref[:, pl.ds(column * head_dim, head_dim)]
        return dot(query, keys[...], ACROSS)

    def finish(column, score):
        lanes = pl.ds(column * head_dim, head_dim)
        before = log_ref[:, lanes]
        top = jnp.maximum(before, jnp.max(score, axis=1, keepdims=True) * scale)
        weight = jnp.concatenate(
            [
                jnp.exp2(score[:, start : start + head_dim] * scale - top).astype(jnp.bfloat16)
                for start in range(0, score.shape[1], head_dim)
            ],
            axis=1,
        )
        mixed = dot(weight, values[...], ALONG)
        share = jnp.exp2(before - top)
        out_ref[:, lanes] = (
            (mixed[:, :head_dim] + mean_ref[:, lanes] * share) / (mixed[:, head_dim:] + share)
        ).astype(out_ref.dtype)

    staggered(range(per_step), scores_of, finish)


def body(queries, suffix_kv, pool_kv, prefix_pages, owner_start, page_slot):
    _, heads, slots, page_len, head_dim = pool_kv.shape
    _, groups, levels = page_slot.shape
    suffix = queries.shape[0]
    per_kv = queries.shape[1] // (heads * head_dim)
    pages = suffix // page_len
    fetched = -(-(levels * groups - pages) // groups)
    page = (2, heads, page_len, head_dim)
    slot_of = jnp.swapaxes(page_slot, 1, 2)
    dtype = pool_kv.dtype

    def exchange(sends):
        arrived = [None] * (groups - 1)
        for step in range(groups - 1, 0, -1):
            pairs = [(index, partner(index, step, groups)[0]) for index in range(groups)]
            arrived[step - 1] = lax.ppermute(sends[step - 1], "pool", pairs)
        return arrived

    own_pages, *sends, gathered = pl.pallas_call(
        fetch_kernel,
        out_shape=[pltpu.VMEM((fetched,) + page, dtype)] * groups
        + [jax.ShapeDtypeStruct((1,), jnp.int32)],
        in_specs=[SMEM, HBM],
        out_specs=[VMEM] * groups + [SMEM],
        scratch_shapes=[pltpu.SemaphoreType.DMA((groups, fetched))],
        name="gather_pages",
    )(slot_of, pool_kv)
    received = exchange(sends)

    per_step = math.gcd(per_kv, 4)
    steps = per_kv // per_step
    scale = math.log2(math.e) / math.sqrt(head_dim)

    def grant(size):
        return pltpu.CompilerParams(vmem_limit_bytes=size * 1024 * 1024)

    total = fetched * groups * page_len
    columns = pl.BlockSpec((suffix, per_step * head_dim), lambda h, s: (0, h * steps + s))
    pages_of = pl.BlockSpec((fetched, 2, 1, page_len, head_dim), lambda h, s: (0, 0, h, 0, 0))

    def cost(keys):
        cells = heads * per_kv * suffix * keys
        return pl.CostEstimate(
            flops=6 * cells * head_dim, bytes_accessed=8 * queries.size, transcendentals=cells
        )

    means, logs, new_pool, own_back, *back_sends = pl.pallas_call(
        functools.partial(suffix_kernel, scale, per_step),
        grid=(heads, steps),
        out_shape=[
            jax.ShapeDtypeStruct(queries.shape, jnp.float32),
            jax.ShapeDtypeStruct(queries.shape, jnp.float32),
            jax.ShapeDtypeStruct(pool_kv.shape, dtype),
        ]
        + [jax.ShapeDtypeStruct(page, dtype)] * groups,
        in_specs=[
            SMEM,
            SMEM,
            SMEM,
            columns,
            pl.BlockSpec((2, 1, suffix, head_dim), lambda h, s: (0, h, 0, 0)),
            pl.BlockSpec((2, 1, slots, page_len, head_dim), lambda h, s: (0, h, 0, 0, 0)),
        ],
        out_specs=[columns, columns, HBM]
        + [pl.BlockSpec((2, 1, page_len, head_dim), lambda h, s: (0, h, 0, 0))] * groups,
        scratch_shapes=[
            pltpu.VMEM((suffix, 2 * head_dim), dtype),
            pltpu.SemaphoreType.DMA(()),
        ],
        compiler_params=grant(60),
        cost_estimate=cost(suffix),
        name="attend_suffix",
    )(prefix_pages, owner_start, gathered, queries, suffix_kv, pool_kv)
    returned = exchange(back_sends)

    result, token = pl.pallas_call(
        functools.partial(prefix_kernel, scale, per_step),
        grid=(heads, steps),
        out_shape=[
            jax.ShapeDtypeStruct(queries.shape, dtype),
            jax.ShapeDtypeStruct((8, head_dim), jnp.float32),
        ],
        in_specs=[
            SMEM,
            SMEM,
            columns,
            columns,
            columns,
        ]
        + [pages_of] * groups,
        out_specs=[columns, pl.BlockSpec((8, head_dim), lambda h, s: (0, 0))],
        scratch_shapes=[
            pltpu.VMEM((total, head_dim), dtype),
            pltpu.VMEM((total, 2 * head_dim), dtype),
        ],
        compiler_params=grant(52),
        cost_estimate=cost(total),
        name="attend_prefix",
    )(prefix_pages, owner_start, queries, means, logs, own_pages, *received)

    new_pool = pl.pallas_call(
        functools.partial(place_kernel, pages),
        out_shape=jax.ShapeDtypeStruct(pool_kv.shape, dtype),
        in_specs=[SMEM, SMEM, SMEM] + [VMEM] * groups + [HBM, HBM],
        out_specs=HBM,
        input_output_aliases={4 + groups: 0},
        scratch_shapes=[pltpu.SemaphoreType.DMA((groups,))],
        compiler_params=grant(50),
        name="place_pages",
    )(prefix_pages, owner_start, slot_of, own_back, *returned, token, new_pool)
    return (result, new_pool)


def solution(mesh):
    in_specs = (
        P(("parts", "pool"), "tp"),
        P(None, "tp", ("parts", "pool"), None),
        P(None, "tp", ("parts", "pool"), None, None),
        P("parts"),
        P("parts"),
        P("parts", None, None),
    )
    out_specs = (P(("parts", "pool"), "tp"), P(None, "tp", ("parts", "pool"), None, None))
    return jax.shard_map(body, mesh=mesh, in_specs=in_specs, out_specs=out_specs, check_vma=False)
```

```python
import functools
import math

import jax
import jax.numpy as jnp
from jax import lax
from jax.experimental import pallas as pl
from jax.experimental.pallas import tpu as pltpu
from jax.sharding import PartitionSpec as P

HBM = pl.BlockSpec(memory_space=pl.ANY)
VMEM = pl.BlockSpec(memory_space=pltpu.VMEM)
SMEM = pl.BlockSpec(memory_space=pltpu.SMEM)
TILE = 256


def partner(index, step, groups):
    if groups & (groups - 1):
        return (index + step) % groups, (index + groups - step) % groups
    return index ^ step, index ^ step


def turn_of(index, source, groups):
    if groups & (groups - 1):
        return lax.rem(index + groups - source, groups)
    return index ^ source


def fetch_kernel(slots_ref, pool_ref, *rest):
    *sends, token_ref, sems = rest
    groups = slots_ref.shape[2]
    levels = sends[0].shape[0]
    me = lax.axis_index("pool")
    copies = []
    for step in range(groups - 1, -1, -1):
        dest = partner(me, step, groups)[0]
        for level in range(levels):
            slot = slots_ref[dest, level, me]
            copies.append(
                pltpu.make_async_copy(
                    pool_ref.at[:, :, slot], sends[step].at[level], sems.at[step, level]
                )
            )
    for copy in copies:
        copy.start()
    token_ref[0] = me
    for copy in copies:
        copy.wait()


def place_kernel(pages, length_ref, start_ref, slots_ref, *rest):
    backs, new_ref, sems = rest[:-4], rest[-2], rest[-1]
    _, levels, groups = slots_ref.shape
    me = lax.axis_index("pool")

    def each(act):
        for step in range(groups):
            request = partner(me, step, groups)[1]
            length = length_ref[request]
            first = lax.rem(start_ref[request] + length, groups)
            offset = lax.rem(me + groups - first, groups)

            @pl.when(offset < pages)
            def _():
                level = jnp.minimum(lax.div(length + offset, groups), levels - 1)
                slot = slots_ref[request, level, me]
                act(
                    pltpu.make_async_copy(backs[step], new_ref.at[:, :, slot], sems.at[step])
                )

    each(lambda copy: copy.start())
    each(lambda copy: copy.wait())


dot = functools.partial(lax.dot_general, preferred_element_type=jnp.float32)
ACROSS = (((1,), (1,)), ((), ()))
ALONG = (((1,), (0,)), ((), ()))


def staggered(items, scores_of, finish):
    ahead = scores_of(items[0])
    for place, item in enumerate(items):
        scores = ahead
        if place + 1 < len(items):
            ahead = scores_of(items[place + 1])
        finish(item, scores)


def suffix_kernel(
    scale, per_step, length_ref, start_ref, _, query_ref, suffix_ref, pool_ref, *rest
):
    mean_ref, log_ref, new_ref, *back_refs, values, sem = rest
    groups = len(back_refs)
    page_len, head_dim = pool_ref.shape[3:]
    suffix = query_ref.shape[0]
    pages = suffix // page_len
    head, step = pl.program_id(0), pl.program_id(1)
    copy = pltpu.make_async_copy(pool_ref, new_ref.at[:, pl.ds(head, 1)], sem)

    @pl.when(step == 0)
    def _():
        copy.start()
        values[:, pl.ds(0, head_dim)] = suffix_ref[1, 0]
        values[:, pl.ds(head_dim, head_dim)] = jnp.ones((suffix, head_dim), values.dtype)
        me = lax.axis_index("pool")
        first = lax.rem(start_ref[me] + length_ref[me], groups)
        for turn in range(groups):
            offset = lax.rem(partner(me, turn, groups)[0] + groups - first, groups)
            row = pl.multiple_of(jnp.minimum(offset, pages - 1) * page_len, page_len)
            for side in range(2):
                back_refs[turn][side, 0] = suffix_ref[side, 0, pl.ds(row, page_len), :]

    tile = min(TILE, suffix)
    seen = lax.broadcasted_iota(jnp.int32, (tile, tile), 1) <= lax.broadcasted_iota(
        jnp.int32, (tile, tile), 0
    )

    def scores_of(column):
        lanes = pl.ds(column * head_dim, head_dim)
        return [
            dot(query_ref[row:, lanes], suffix_ref[0, 0, pl.ds(row, tile), :], ACROSS)
            for row in range(0, suffix, tile)
        ]

    def finish(column, scores):
        lanes = pl.ds(column * head_dim, head_dim)
        scores = [
            [
                block[row : row + tile] if row else jnp.where(seen, block[:tile], -jnp.inf)
                for row in range(0, block.shape[0], tile)
            ]
            for block in scores
        ]
        blocks = len(scores)
        tops = [
            functools.reduce(
                jnp.maximum,
                [
                    jnp.max(scores[key][row - key], axis=1, keepdims=True)
                    for key in range(row + 1)
                ],
            )
            for row in range(blocks)
        ]
        mixed = [None] * blocks
        for key in range(blocks):
            weight = [
                jnp.exp2((scores[key][row - key] - tops[row]) * scale).astype(jnp.bfloat16)
                for row in range(key, blocks)
            ]
            weight = jnp.concatenate(weight, axis=0) if len(weight) > 1 else weight[0]
            part = dot(weight, values[pl.ds(key * tile, tile), :], ALONG)
            for row in range(key, blocks):
                piece = part[(row - key) * tile : (row - key + 1) * tile]
                mixed[row] = piece if mixed[row] is None else mixed[row] + piece
        for row in range(blocks):
            rows = pl.ds(row * tile, tile)
            count = mixed[row][:, head_dim:]
            mean_ref[rows, lanes] = mixed[row][:, :head_dim] / count
            log_ref[rows, lanes] = tops[row] * scale + jnp.log2(count)

    staggered(range(per_step), scores_of, finish)

    @pl.when(step == pl.num_programs(1) - 1)
    def _():
        copy.wait()


def prefix_kernel(
    scale, per_step, length_ref, start_ref, query_ref, mean_ref, log_ref, *rest
):
    *page_refs, out_ref, token_ref, keys, values = rest
    groups = len(page_refs)
    levels, _, _, page_len, head_dim = page_refs[0].shape
    suffix = query_ref.shape[0]

    token_ref[...] = jnp.zeros_like(token_ref)

    @pl.when(pl.program_id(1) == 0)
    def _():
        me = lax.axis_index("pool")
        length, first = length_ref[me], start_ref[me]
        places = []
        for turn in range(groups):
            owner = partner(me, turn, groups)[1]
            for level in range(levels):
                rows = pl.ds((turn * levels + level) * page_len, page_len)
                seen = level * groups + lax.rem(owner + groups - first, groups) < length
                places.append((rows, seen))
                keys[rows, :] = page_refs[turn][level, 0, 0]

                @pl.when(seen)
                def _():
                    values[rows, pl.ds(0, head_dim)] = page_refs[turn][level, 1, 0]
                    values[rows, pl.ds(head_dim, head_dim)] = jnp.ones(
                        (page_len, head_dim), values.dtype
                    )

        page_zero = pl.ds(
            pl.multiple_of(turn_of(me, first, groups) * levels * page_len, page_len), page_len
        )
        for rows, seen in places:

            @pl.when(jnp.logical_not(seen))
            def _():
                keys[rows, :] = keys[page_zero, :]
                values[rows, :] = jnp.zeros((page_len, 2 * head_dim), values.dtype)

    def scores_of(column):
        query = query_ref[:, pl.ds(column * head_dim, head_dim)]
        return dot(query, keys[...], ACROSS)

    def finish(column, score):
        lanes = pl.ds(column * head_dim, head_dim)
        before = log_ref[:, lanes]
        top = jnp.maximum(before, jnp.max(score, axis=1, keepdims=True) * scale)
        weight = jnp.concatenate(
            [
                jnp.exp2(score[:, start : start + head_dim] * scale - top).astype(jnp.bfloat16)
                for start in range(0, score.shape[1], head_dim)
            ],
            axis=1,
        )
        mixed = dot(weight, values[...], ALONG)
        share = jnp.exp2(before - top)
        out_ref[:, lanes] = (
            (mixed[:, :head_dim] + mean_ref[:, lanes] * share) / (mixed[:, head_dim:] + share)
        ).astype(out_ref.dtype)

    staggered(range(per_step), scores_of, finish)


def body(queries, suffix_kv, pool_kv, prefix_pages, owner_start, page_slot):
    _, heads, slots, page_len, head_dim = pool_kv.shape
    _, groups, levels = page_slot.shape
    suffix = queries.shape[0]
    per_kv = queries.shape[1] // (heads * head_dim)
    pages = suffix // page_len
    fetched = -(-(levels * groups - pages) // groups)
    page = (2, heads, page_len, head_dim)
    slot_of = jnp.swapaxes(page_slot, 1, 2)
    dtype = pool_kv.dtype

    def exchange(sends):
        arrived = [None] * (groups - 1)
        for step in range(groups - 1, 0, -1):
            pairs = [(index, partner(index, step, groups)[0]) for index in range(groups)]
            arrived[step - 1] = lax.ppermute(sends[step - 1], "pool", pairs)
        return arrived

    own_pages, *sends, gathered = pl.pallas_call(
        fetch_kernel,
        out_shape=[pltpu.VMEM((fetched,) + page, dtype)] * groups
        + [jax.ShapeDtypeStruct((1,), jnp.int32)],
        in_specs=[SMEM, HBM],
        out_specs=[VMEM] * groups + [SMEM],
        scratch_shapes=[pltpu.SemaphoreType.DMA((groups, fetched))],
        name="gather_pages",
    )(slot_of, pool_kv)
    received = exchange(sends)

    per_step = math.gcd(per_kv, 2)
    steps = per_kv // per_step
    scale = math.log2(math.e) / math.sqrt(head_dim)

    def grant(size):
        return pltpu.CompilerParams(vmem_limit_bytes=size * 1024 * 1024)

    total = fetched * groups * page_len
    columns = pl.BlockSpec((suffix, per_step * head_dim), lambda h, s: (0, h * steps + s))
    pages_of = pl.BlockSpec((fetched, 2, 1, page_len, head_dim), lambda h, s: (0, 0, h, 0, 0))

    def cost(keys):
        cells = heads * per_kv * suffix * keys
        return pl.CostEstimate(
            flops=6 * cells * head_dim, bytes_accessed=8 * queries.size, transcendentals=cells
        )

    means, logs, new_pool, own_back, *back_sends = pl.pallas_call(
        functools.partial(suffix_kernel, scale, per_step),
        grid=(heads, steps),
        out_shape=[
            jax.ShapeDtypeStruct(queries.shape, jnp.float32),
            jax.ShapeDtypeStruct(queries.shape, jnp.float32),
            jax.ShapeDtypeStruct(pool_kv.shape, dtype),
        ]
        + [jax.ShapeDtypeStruct(page, dtype)] * groups,
        in_specs=[
            SMEM,
            SMEM,
            SMEM,
            columns,
            pl.BlockSpec((2, 1, suffix, head_dim), lambda h, s: (0, h, 0, 0)),
            pl.BlockSpec((2, 1, slots, page_len, head_dim), lambda h, s: (0, h, 0, 0, 0)),
        ],
        out_specs=[columns, columns, HBM]
        + [pl.BlockSpec((2, 1, page_len, head_dim), lambda h, s: (0, h, 0, 0))] * groups,
        scratch_shapes=[
            pltpu.VMEM((suffix, 2 * head_dim), dtype),
            pltpu.SemaphoreType.DMA(()),
        ],
        compiler_params=grant(60),
        cost_estimate=cost(suffix),
        name="attend_suffix",
    )(prefix_pages, owner_start, gathered, queries, suffix_kv, pool_kv)
    returned = exchange(back_sends)

    result, token = pl.pallas_call(
        functools.partial(prefix_kernel, scale, per_step),
        grid=(heads, steps),
        out_shape=[
            jax.ShapeDtypeStruct(queries.shape, dtype),
            jax.ShapeDtypeStruct((8, head_dim), jnp.float32),
        ],
        in_specs=[
            SMEM,
            SMEM,
            columns,
            columns,
            columns,
        ]
        + [pages_of] * groups,
        out_specs=[columns, pl.BlockSpec((8, head_dim), lambda h, s: (0, 0))],
        scratch_shapes=[
            pltpu.VMEM((total, head_dim), dtype),
            pltpu.VMEM((total, 2 * head_dim), dtype),
        ],
        compiler_params=grant(52),
        cost_estimate=cost(total),
        name="attend_prefix",
    )(prefix_pages, owner_start, queries, means, logs, own_pages, *received)

    new_pool = pl.pallas_call(
        functools.partial(place_kernel, pages),
        out_shape=jax.ShapeDtypeStruct(pool_kv.shape, dtype),
        in_specs=[SMEM, SMEM, SMEM] + [VMEM] * groups + [HBM, HBM],
        out_specs=HBM,
        input_output_aliases={4 + groups: 0},
        scratch_shapes=[pltpu.SemaphoreType.DMA((groups,))],
        compiler_params=grant(50),
        name="place_pages",
    )(prefix_pages, owner_start, slot_of, own_back, *returned, token, new_pool)
    return (result, new_pool)


def solution(mesh):
    in_specs = (
        P(("parts", "pool"), "tp"),
        P(None, "tp", ("parts", "pool"), None),
        P(None, "tp", ("parts", "pool"), None, None),
        P("parts"),
        P("parts"),
        P("parts", None, None),
    )
    out_specs = (P(("parts", "pool"), "tp"), P(None, "tp", ("parts", "pool"), None, None))
    return jax.shard_map(body, mesh=mesh, in_specs=in_specs, out_specs=out_specs, check_vma=False)
```

```python
import functools
import math

import jax
import jax.numpy as jnp
from jax import lax
from jax.experimental import pallas as pl
from jax.experimental.pallas import tpu as pltpu
from jax.sharding import PartitionSpec as P

HBM = pl.BlockSpec(memory_space=pl.ANY)
VMEM = pl.BlockSpec(memory_space=pltpu.VMEM)
SMEM = pl.BlockSpec(memory_space=pltpu.SMEM)
TILE = 256


def partner(index, step, groups):
    if groups & (groups - 1):
        return (index + step) % groups, (index + groups - step) % groups
    return index ^ step, index ^ step


def turn_of(index, source, groups):
    if groups & (groups - 1):
        return lax.rem(index + groups - source, groups)
    return index ^ source


def fetch_kernel(slots_ref, pool_ref, *rest):
    *sends, token_ref, sems = rest
    groups = slots_ref.shape[2]
    levels = sends[0].shape[0]
    me = lax.axis_index("pool")
    copies = []
    for step in range(groups - 1, -1, -1):
        dest = partner(me, step, groups)[0]
        for level in range(levels):
            slot = slots_ref[dest, level, me]
            copies.append(
                pltpu.make_async_copy(
                    pool_ref.at[:, :, slot], sends[step].at[level], sems.at[step, level]
                )
            )
    for copy in copies:
        copy.start()
    token_ref[0] = me
    for copy in copies:
        copy.wait()


def place_kernel(pages, length_ref, start_ref, slots_ref, *rest):
    backs, new_ref, sems = rest[:-4], rest[-2], rest[-1]
    _, levels, groups = slots_ref.shape
    me = lax.axis_index("pool")

    def each(act):
        for step in range(groups):
            request = partner(me, step, groups)[1]
            length = length_ref[request]
            first = lax.rem(start_ref[request] + length, groups)
            offset = lax.rem(me + groups - first, groups)

            @pl.when(offset < pages)
            def _():
                level = jnp.minimum(lax.div(length + offset, groups), levels - 1)
                slot = slots_ref[request, level, me]
                act(
                    pltpu.make_async_copy(backs[step], new_ref.at[:, :, slot], sems.at[step])
                )

    each(lambda copy: copy.start())
    each(lambda copy: copy.wait())


dot = functools.partial(lax.dot_general, preferred_element_type=jnp.float32)
ACROSS = (((1,), (1,)), ((), ()))
ALONG = (((1,), (0,)), ((), ()))


def staggered(items, scores_of, finish):
    ahead = scores_of(items[0])
    for place, item in enumerate(items):
        scores = ahead
        if place + 1 < len(items):
            ahead = scores_of(items[place + 1])
        finish(item, scores)


def suffix_kernel(
    scale, per_step, length_ref, start_ref, _, query_ref, suffix_ref, pool_ref, *rest
):
    mean_out, log_out, new_ref, *back_refs, means, logs, values, sem, sems = rest
    groups = len(back_refs)
    page_len, head_dim = pool_ref.shape[3:]
    suffix = query_ref.shape[0]
    pages = suffix // page_len
    head, step = pl.program_id(0), pl.program_id(1)
    copy = pltpu.make_async_copy(pool_ref, new_ref.at[:, pl.ds(head, 1)], sem)
    turn_now = head * pl.num_programs(1) + step

    def leaving(column):
        place = step * per_step + column
        return [
            pltpu.make_async_copy(means.at[column], mean_out.at[head, place], sems.at[0, column]),
            pltpu.make_async_copy(logs.at[column], log_out.at[head, place], sems.at[1, column]),
        ]

    def wait_leaving():
        for column in range(per_step):
            for part in leaving(column):
                part.wait()

    @pl.when(turn_now > 0)
    def _():
        wait_leaving()

    @pl.when(step == 0)
    def _():
        copy.start()
        values[:, pl.ds(0, head_dim)] = suffix_ref[1, 0]
        values[:, pl.ds(head_dim, head_dim)] = jnp.ones((suffix, head_dim), values.dtype)
        me = lax.axis_index("pool")
        first = lax.rem(start_ref[me] + length_ref[me], groups)
        for turn in range(groups):
            offset = lax.rem(partner(me, turn, groups)[0] + groups - first, groups)
            row = pl.multiple_of(jnp.minimum(offset, pages - 1) * page_len, page_len)
            for side in range(2):
                back_refs[turn][side, 0] = suffix_ref[side, 0, pl.ds(row, page_len), :]

    tile = min(TILE, suffix)
    seen = lax.broadcasted_iota(jnp.int32, (tile, tile), 1) <= lax.broadcasted_iota(
        jnp.int32, (tile, tile), 0
    )

    def scores_of(column):
        lanes = pl.ds(column * head_dim, head_dim)
        return [
            dot(query_ref[row:, lanes], suffix_ref[0, 0, pl.ds(row, tile), :], ACROSS)
            for row in range(0, suffix, tile)
        ]

    def finish(column, scores):
        scores = [
            [
                block[row : row + tile] if row else jnp.where(seen, block[:tile], -jnp.inf)
                for row in range(0, block.shape[0], tile)
            ]
            for block in scores
        ]
        blocks = len(scores)
        tops = [
            functools.reduce(
                jnp.maximum,
                [
                    jnp.max(scores[key][row - key], axis=1, keepdims=True)
                    for key in range(row + 1)
                ],
            )
            for row in range(blocks)
        ]
        mixed = [None] * blocks
        for key in range(blocks):
            weight = [
                jnp.exp2((scores[key][row - key] - tops[row]) * scale).astype(jnp.bfloat16)
                for row in range(key, blocks)
            ]
            weight = jnp.concatenate(weight, axis=0) if len(weight) > 1 else weight[0]
            part = dot(weight, values[pl.ds(key * tile, tile), :], ALONG)
            for row in range(key, blocks):
                piece = part[(row - key) * tile : (row - key + 1) * tile]
                mixed[row] = piece if mixed[row] is None else mixed[row] + piece
        for row in range(blocks):
            rows = pl.ds(row * tile, tile)
            count = mixed[row][:, head_dim:]
            means[column, rows, :] = mixed[row][:, :head_dim] / count
            logs[column, rows, :] = tops[row] * scale + jnp.log2(count)
        for part in leaving(column):
            part.start()

    staggered(range(per_step), scores_of, finish)

    @pl.when(step == pl.num_programs(1) - 1)
    def _():
        copy.wait()

    @pl.when(turn_now == pl.num_programs(0) * pl.num_programs(1) - 1)
    def _():
        wait_leaving()


def prefix_kernel(
    scale, per_step, length_ref, start_ref, query_ref, mean_ref, log_ref, *rest
):
    *page_refs, out_ref, token_ref, keys, values = rest
    groups = len(page_refs)
    levels, _, _, page_len, head_dim = page_refs[0].shape
    suffix = query_ref.shape[0]

    token_ref[...] = jnp.zeros_like(token_ref)

    @pl.when(pl.program_id(1) == 0)
    def _():
        me = lax.axis_index("pool")
        length, first = length_ref[me], start_ref[me]
        places = []
        for turn in range(groups):
            owner = partner(me, turn, groups)[1]
            for level in range(levels):
                rows = pl.ds((turn * levels + level) * page_len, page_len)
                seen = level * groups + lax.rem(owner + groups - first, groups) < length
                places.append((rows, seen))
                keys[rows, :] = page_refs[turn][level, 0, 0]

                @pl.when(seen)
                def _():
                    values[rows, pl.ds(0, head_dim)] = page_refs[turn][level, 1, 0]
                    values[rows, pl.ds(head_dim, head_dim)] = jnp.ones(
                        (page_len, head_dim), values.dtype
                    )

        page_zero = pl.ds(
            pl.multiple_of(turn_of(me, first, groups) * levels * page_len, page_len), page_len
        )
        for rows, seen in places:

            @pl.when(jnp.logical_not(seen))
            def _():
                keys[rows, :] = keys[page_zero, :]
                values[rows, :] = jnp.zeros((page_len, 2 * head_dim), values.dtype)

    def scores_of(column):
        query = query_ref[:, pl.ds(column * head_dim, head_dim)]
        return dot(query, keys[...], ACROSS)

    def finish(column, score):
        lanes = pl.ds(column * head_dim, head_dim)
        before = log_ref[0, column]
        top = jnp.maximum(before, jnp.max(score, axis=1, keepdims=True) * scale)
        weight = jnp.concatenate(
            [
                jnp.exp2(score[:, start : start + head_dim] * scale - top).astype(jnp.bfloat16)
                for start in range(0, score.shape[1], head_dim)
            ],
            axis=1,
        )
        mixed = dot(weight, values[...], ALONG)
        share = jnp.exp2(before - top)
        out_ref[:, lanes] = (
            (mixed[:, :head_dim] + mean_ref[0, column] * share) / (mixed[:, head_dim:] + share)
        ).astype(out_ref.dtype)

    staggered(range(per_step), scores_of, finish)


def body(queries, suffix_kv, pool_kv, prefix_pages, owner_start, page_slot):
    _, heads, slots, page_len, head_dim = pool_kv.shape
    _, groups, levels = page_slot.shape
    suffix = queries.shape[0]
    per_kv = queries.shape[1] // (heads * head_dim)
    pages = suffix // page_len
    fetched = -(-(levels * groups - pages) // groups)
    page = (2, heads, page_len, head_dim)
    slot_of = jnp.swapaxes(page_slot, 1, 2)
    dtype = pool_kv.dtype

    def exchange(sends):
        arrived = [None] * (groups - 1)
        for step in range(groups - 1, 0, -1):
            pairs = [(index, partner(index, step, groups)[0]) for index in range(groups)]
            arrived[step - 1] = lax.ppermute(sends[step - 1], "pool", pairs)
        return arrived

    own_pages, *sends, gathered = pl.pallas_call(
        fetch_kernel,
        out_shape=[pltpu.VMEM((fetched,) + page, dtype)] * groups
        + [jax.ShapeDtypeStruct((1,), jnp.int32)],
        in_specs=[SMEM, HBM],
        out_specs=[VMEM] * groups + [SMEM],
        scratch_shapes=[pltpu.SemaphoreType.DMA((groups, fetched))],
        name="gather_pages",
    )(slot_of, pool_kv)
    received = exchange(sends)

    per_step = math.gcd(per_kv, 4)
    steps = per_kv // per_step
    scale = math.log2(math.e) / math.sqrt(head_dim)

    def grant(size):
        return pltpu.CompilerParams(vmem_limit_bytes=size * 1024 * 1024)

    total = fetched * groups * page_len
    columns = pl.BlockSpec((suffix, per_step * head_dim), lambda h, s: (0, h * steps + s))
    per_head = pl.BlockSpec((1, per_step, suffix, head_dim), lambda h, s: (h, s, 0, 0))
    pages_of = pl.BlockSpec((fetched, 2, 1, page_len, head_dim), lambda h, s: (0, 0, h, 0, 0))

    def cost(keys):
        cells = heads * per_kv * suffix * keys
        return pl.CostEstimate(
            flops=6 * cells * head_dim, bytes_accessed=8 * queries.size, transcendentals=cells
        )

    means, logs, new_pool, own_back, *back_sends = pl.pallas_call(
        functools.partial(suffix_kernel, scale, per_kv),
        grid=(heads, 1),
        out_shape=[
            jax.ShapeDtypeStruct((heads, per_kv, suffix, head_dim), jnp.float32),
            jax.ShapeDtypeStruct((heads, per_kv, suffix, head_dim), jnp.float32),
            jax.ShapeDtypeStruct(pool_kv.shape, dtype),
        ]
        + [jax.ShapeDtypeStruct(page, dtype)] * groups,
        in_specs=[
            SMEM,
            SMEM,
            SMEM,
            pl.BlockSpec((suffix, per_kv * head_dim), lambda h, s: (0, h)),
            pl.BlockSpec((2, 1, suffix, head_dim), lambda h, s: (0, h, 0, 0)),
            pl.BlockSpec((2, 1, slots, page_len, head_dim), lambda h, s: (0, h, 0, 0, 0)),
        ],
        out_specs=[HBM, HBM, HBM]
        + [pl.BlockSpec((2, 1, page_len, head_dim), lambda h, s: (0, h, 0, 0))] * groups,
        scratch_shapes=[
            pltpu.VMEM((per_kv, suffix, head_dim), jnp.float32),
            pltpu.VMEM((per_kv, suffix, head_dim), jnp.float32),
            pltpu.VMEM((suffix, 2 * head_dim), dtype),
            pltpu.SemaphoreType.DMA(()),
            pltpu.SemaphoreType.DMA((2, per_kv)),
        ],
        compiler_params=grant(60),
        cost_estimate=cost(suffix),
        name="attend_suffix",
    )(prefix_pages, owner_start, gathered, queries, suffix_kv, pool_kv)
    returned = exchange(back_sends)

    result, token = pl.pallas_call(
        functools.partial(prefix_kernel, scale, per_step),
        grid=(heads, steps),
        out_shape=[
            jax.ShapeDtypeStruct(queries.shape, dtype),
            jax.ShapeDtypeStruct((8, head_dim), jnp.float32),
        ],
        in_specs=[
            SMEM,
            SMEM,
            columns,
            per_head,
            per_head,
        ]
        + [pages_of] * groups,
        out_specs=[columns, pl.BlockSpec((8, head_dim), lambda h, s: (0, 0))],
        scratch_shapes=[
            pltpu.VMEM((total, head_dim), dtype),
            pltpu.VMEM((total, 2 * head_dim), dtype),
        ],
        compiler_params=grant(52),
        cost_estimate=cost(total),
        name="attend_prefix",
    )(prefix_pages, owner_start, queries, means, logs, own_pages, *received)

    new_pool = pl.pallas_call(
        functools.partial(place_kernel, pages),
        out_shape=jax.ShapeDtypeStruct(pool_kv.shape, dtype),
        in_specs=[SMEM, SMEM, SMEM] + [VMEM] * groups + [HBM, HBM],
        out_specs=HBM,
        input_output_aliases={4 + groups: 0},
        scratch_shapes=[pltpu.SemaphoreType.DMA((groups,))],
        compiler_params=grant(50),
        name="place_pages",
    )(prefix_pages, owner_start, slot_of, own_back, *returned, token, new_pool)
    return (result, new_pool)


def solution(mesh):
    in_specs = (
        P(("parts", "pool"), "tp"),
        P(None, "tp", ("parts", "pool"), None),
        P(None, "tp", ("parts", "pool"), None, None),
        P("parts"),
        P("parts"),
        P("parts", None, None),
    )
    out_specs = (P(("parts", "pool"), "tp"), P(None, "tp", ("parts", "pool"), None, None))
    return jax.shard_map(body, mesh=mesh, in_specs=in_specs, out_specs=out_specs, check_vma=False)
```

```python
import functools
import math

import jax
import jax.numpy as jnp
from jax import lax
from jax.experimental import pallas as pl
from jax.experimental.pallas import tpu as pltpu
from jax.sharding import PartitionSpec as P

HBM = pl.BlockSpec(memory_space=pl.ANY)
VMEM = pl.BlockSpec(memory_space=pltpu.VMEM)
SMEM = pl.BlockSpec(memory_space=pltpu.SMEM)
TILE = 256


def partner(index, step, groups):
    if groups & (groups - 1):
        return (index + step) % groups, (index + groups - step) % groups
    return index ^ step, index ^ step


def turn_of(index, source, groups):
    if groups & (groups - 1):
        return lax.rem(index + groups - source, groups)
    return index ^ source


def fetch_kernel(slots_ref, pool_ref, *rest):
    *sends, token_ref, sems = rest
    groups = slots_ref.shape[2]
    levels = sends[0].shape[0]
    me = lax.axis_index("pool")
    copies = []
    for step in range(groups - 1, -1, -1):
        dest = partner(me, step, groups)[0]
        for level in range(levels):
            slot = slots_ref[dest, level, me]
            copies.append(
                pltpu.make_async_copy(
                    pool_ref.at[:, :, slot], sends[step].at[level], sems.at[step, level]
                )
            )
    for copy in copies:
        copy.start()
    token_ref[0] = me
    for copy in copies:
        copy.wait()


def place_kernel(pages, length_ref, start_ref, slots_ref, *rest):
    backs, new_ref, sems = rest[:-4], rest[-2], rest[-1]
    _, levels, groups = slots_ref.shape
    me = lax.axis_index("pool")

    def each(act):
        for step in range(groups):
            request = partner(me, step, groups)[1]
            length = length_ref[request]
            first = lax.rem(start_ref[request] + length, groups)
            offset = lax.rem(me + groups - first, groups)

            @pl.when(offset < pages)
            def _():
                level = jnp.minimum(lax.div(length + offset, groups), levels - 1)
                slot = slots_ref[request, level, me]
                act(
                    pltpu.make_async_copy(backs[step], new_ref.at[:, :, slot], sems.at[step])
                )

    each(lambda copy: copy.start())
    each(lambda copy: copy.wait())


dot = functools.partial(lax.dot_general, preferred_element_type=jnp.float32)
ACROSS = (((1,), (1,)), ((), ()))
ALONG = (((1,), (0,)), ((), ()))


def staggered(items, scores_of, finish):
    ahead = scores_of(items[0])
    for place, item in enumerate(items):
        scores = ahead
        if place + 1 < len(items):
            ahead = scores_of(items[place + 1])
        finish(item, scores)


def suffix_kernel(
    scale, per_step, length_ref, start_ref, _, query_ref, suffix_ref, pool_ref, *rest
):
    mean_out, log_out, new_ref, *back_refs, means, logs, values, sem, sems = rest
    groups = len(back_refs)
    page_len, head_dim = pool_ref.shape[3:]
    suffix = query_ref.shape[0]
    pages = suffix // page_len
    head, step = pl.program_id(0), pl.program_id(1)
    copy = pltpu.make_async_copy(pool_ref, new_ref.at[:, pl.ds(head, 1)], sem)
    turn_now = head * pl.num_programs(1) + step

    def leaving(column):
        place = step * per_step + column
        return [
            pltpu.make_async_copy(means.at[column], mean_out.at[head, place], sems.at[0, column]),
            pltpu.make_async_copy(logs.at[column], log_out.at[head, place], sems.at[1, column]),
        ]

    def wait_leaving():
        for column in range(per_step):
            for part in leaving(column):
                part.wait()

    @pl.when(turn_now > 0)
    def _():
        wait_leaving()

    @pl.when(step == 0)
    def _():
        copy.start()
        values[:, pl.ds(0, head_dim)] = suffix_ref[1, 0]
        values[:, pl.ds(head_dim, head_dim)] = jnp.ones((suffix, head_dim), values.dtype)
        me = lax.axis_index("pool")
        first = lax.rem(start_ref[me] + length_ref[me], groups)
        for turn in range(groups):
            offset = lax.rem(partner(me, turn, groups)[0] + groups - first, groups)
            row = pl.multiple_of(jnp.minimum(offset, pages - 1) * page_len, page_len)
            for side in range(2):
                back_refs[turn][side, 0] = suffix_ref[side, 0, pl.ds(row, page_len), :]

    tile = min(TILE, suffix)
    seen = lax.broadcasted_iota(jnp.int32, (tile, tile), 1) <= lax.broadcasted_iota(
        jnp.int32, (tile, tile), 0
    )

    def scores_of(column):
        lanes = pl.ds(column * head_dim, head_dim)
        return [
            dot(query_ref[row:, lanes], suffix_ref[0, 0, pl.ds(row, tile), :], ACROSS)
            for row in range(0, suffix, tile)
        ]

    def finish(column, scores):
        scores = [
            [
                block[row : row + tile] if row else jnp.where(seen, block[:tile], -jnp.inf)
                for row in range(0, block.shape[0], tile)
            ]
            for block in scores
        ]
        blocks = len(scores)
        tops = [
            functools.reduce(
                jnp.maximum,
                [
                    jnp.max(scores[key][row - key], axis=1, keepdims=True)
                    for key in range(row + 1)
                ],
            )
            for row in range(blocks)
        ]
        mixed = [None] * blocks
        for key in range(blocks):
            weight = [
                jnp.exp2((scores[key][row - key] - tops[row]) * scale).astype(jnp.bfloat16)
                for row in range(key, blocks)
            ]
            weight = jnp.concatenate(weight, axis=0) if len(weight) > 1 else weight[0]
            part = dot(weight, values[pl.ds(key * tile, tile), :], ALONG)
            for row in range(key, blocks):
                piece = part[(row - key) * tile : (row - key + 1) * tile]
                mixed[row] = piece if mixed[row] is None else mixed[row] + piece
        for row in range(blocks):
            rows = pl.ds(row * tile, tile)
            count = mixed[row][:, head_dim:]
            means[column, rows, :] = mixed[row][:, :head_dim] / count
            logs[column, rows, :] = tops[row] * scale + jnp.log2(count)
        for part in leaving(column):
            part.start()

    staggered(range(per_step), scores_of, finish)

    @pl.when(step == pl.num_programs(1) - 1)
    def _():
        copy.wait()

    @pl.when(turn_now == pl.num_programs(0) * pl.num_programs(1) - 1)
    def _():
        wait_leaving()


def prefix_kernel(
    scale, per_step, length_ref, start_ref, query_ref, mean_ref, log_ref, *rest
):
    *page_refs, out_ref, token_ref, keys, values = rest
    groups = len(page_refs)
    levels, _, _, page_len, head_dim = page_refs[0].shape
    suffix = query_ref.shape[0]

    token_ref[...] = jnp.zeros_like(token_ref)

    @pl.when(pl.program_id(1) == 0)
    def _():
        me = lax.axis_index("pool")
        length, first = length_ref[me], start_ref[me]
        places = []
        for turn in range(groups):
            owner = partner(me, turn, groups)[1]
            for level in range(levels):
                rows = pl.ds((turn * levels + level) * page_len, page_len)
                seen = level * groups + lax.rem(owner + groups - first, groups) < length
                places.append((rows, seen))
                keys[rows, :] = page_refs[turn][level, 0, 0]

                @pl.when(seen)
                def _():
                    values[rows, pl.ds(0, head_dim)] = page_refs[turn][level, 1, 0]
                    values[rows, pl.ds(head_dim, head_dim)] = jnp.ones(
                        (page_len, head_dim), values.dtype
                    )

        page_zero = pl.ds(
            pl.multiple_of(turn_of(me, first, groups) * levels * page_len, page_len), page_len
        )
        for rows, seen in places:

            @pl.when(jnp.logical_not(seen))
            def _():
                keys[rows, :] = keys[page_zero, :]
                values[rows, :] = jnp.zeros((page_len, 2 * head_dim), values.dtype)

    def scores_of(column):
        query = query_ref[:, pl.ds(column * head_dim, head_dim)]
        return dot(query, keys[...], ACROSS)

    def finish(column, score):
        lanes = pl.ds(column * head_dim, head_dim)
        before = log_ref[0, column]
        top = jnp.maximum(before, jnp.max(score, axis=1, keepdims=True) * scale)
        weight = jnp.concatenate(
            [
                jnp.exp2(score[:, start : start + head_dim] * scale - top).astype(jnp.bfloat16)
                for start in range(0, score.shape[1], head_dim)
            ],
            axis=1,
        )
        mixed = dot(weight, values[...], ALONG)
        share = jnp.exp2(before - top)
        out_ref[:, lanes] = (
            (mixed[:, :head_dim] + mean_ref[0, column] * share) / (mixed[:, head_dim:] + share)
        ).astype(out_ref.dtype)

    staggered(range(per_step), scores_of, finish)


def body(queries, suffix_kv, pool_kv, prefix_pages, owner_start, page_slot):
    _, heads, slots, page_len, head_dim = pool_kv.shape
    _, groups, levels = page_slot.shape
    suffix = queries.shape[0]
    per_kv = queries.shape[1] // (heads * head_dim)
    pages = suffix // page_len
    fetched = -(-(levels * groups - pages) // groups)
    page = (2, heads, page_len, head_dim)
    slot_of = jnp.swapaxes(page_slot, 1, 2)
    dtype = pool_kv.dtype

    def exchange(sends):
        arrived = [None] * (groups - 1)
        for step in range(groups - 1, 0, -1):
            pairs = [(index, partner(index, step, groups)[0]) for index in range(groups)]
            arrived[step - 1] = lax.ppermute(sends[step - 1], "pool", pairs)
        return arrived

    own_pages, *sends, gathered = pl.pallas_call(
        fetch_kernel,
        out_shape=[pltpu.VMEM((fetched,) + page, dtype)] * groups
        + [jax.ShapeDtypeStruct((1,), jnp.int32)],
        in_specs=[SMEM, HBM],
        out_specs=[VMEM] * groups + [SMEM],
        scratch_shapes=[pltpu.SemaphoreType.DMA((groups, fetched))],
        name="gather_pages",
    )(slot_of, pool_kv)
    received = exchange(sends)

    per_step = math.gcd(per_kv, 8)
    steps = per_kv // per_step
    scale = math.log2(math.e) / math.sqrt(head_dim)

    def grant(size):
        return pltpu.CompilerParams(vmem_limit_bytes=size * 1024 * 1024)

    total = fetched * groups * page_len
    columns = pl.BlockSpec((suffix, per_step * head_dim), lambda h, s: (0, h * steps + s))
    per_head = pl.BlockSpec((1, per_step, suffix, head_dim), lambda h, s: (h, s, 0, 0))
    pages_of = pl.BlockSpec((fetched, 2, 1, page_len, head_dim), lambda h, s: (0, 0, h, 0, 0))

    def cost(keys):
        cells = heads * per_kv * suffix * keys
        return pl.CostEstimate(
            flops=6 * cells * head_dim, bytes_accessed=8 * queries.size, transcendentals=cells
        )

    means, logs, new_pool, own_back, *back_sends = pl.pallas_call(
        functools.partial(suffix_kernel, scale, per_kv),
        grid=(heads, 1),
        out_shape=[
            jax.ShapeDtypeStruct((heads, per_kv, suffix, head_dim), jnp.float32),
            jax.ShapeDtypeStruct((heads, per_kv, suffix, head_dim), jnp.float32),
            jax.ShapeDtypeStruct(pool_kv.shape, dtype),
        ]
        + [jax.ShapeDtypeStruct(page, dtype)] * groups,
        in_specs=[
            SMEM,
            SMEM,
            SMEM,
            pl.BlockSpec((suffix, per_kv * head_dim), lambda h, s: (0, h)),
            pl.BlockSpec((2, 1, suffix, head_dim), lambda h, s: (0, h, 0, 0)),
            pl.BlockSpec((2, 1, slots, page_len, head_dim), lambda h, s: (0, h, 0, 0, 0)),
        ],
        out_specs=[HBM, HBM, HBM]
        + [pl.BlockSpec((2, 1, page_len, head_dim), lambda h, s: (0, h, 0, 0))] * groups,
        scratch_shapes=[
            pltpu.VMEM((per_kv, suffix, head_dim), jnp.float32),
            pltpu.VMEM((per_kv, suffix, head_dim), jnp.float32),
            pltpu.VMEM((suffix, 2 * head_dim), dtype),
            pltpu.SemaphoreType.DMA(()),
            pltpu.SemaphoreType.DMA((2, per_kv)),
        ],
        compiler_params=grant(60),
        cost_estimate=cost(suffix),
        name="attend_suffix",
    )(prefix_pages, owner_start, gathered, queries, suffix_kv, pool_kv)
    returned = exchange(back_sends)

    result, token = pl.pallas_call(
        functools.partial(prefix_kernel, scale, per_step),
        grid=(heads, steps),
        out_shape=[
            jax.ShapeDtypeStruct(queries.shape, dtype),
            jax.ShapeDtypeStruct((8, head_dim), jnp.float32),
        ],
        in_specs=[
            SMEM,
            SMEM,
            columns,
            per_head,
            per_head,
        ]
        + [pages_of] * groups,
        out_specs=[columns, pl.BlockSpec((8, head_dim), lambda h, s: (0, 0))],
        scratch_shapes=[
            pltpu.VMEM((total, head_dim), dtype),
            pltpu.VMEM((total, 2 * head_dim), dtype),
        ],
        compiler_params=grant(52),
        cost_estimate=cost(total),
        name="attend_prefix",
    )(prefix_pages, owner_start, queries, means, logs, own_pages, *received)

    new_pool = pl.pallas_call(
        functools.partial(place_kernel, pages),
        out_shape=jax.ShapeDtypeStruct(pool_kv.shape, dtype),
        in_specs=[SMEM, SMEM, SMEM] + [VMEM] * groups + [HBM, HBM],
        out_specs=HBM,
        input_output_aliases={4 + groups: 0},
        scratch_shapes=[pltpu.SemaphoreType.DMA((groups,))],
        compiler_params=grant(50),
        name="place_pages",
    )(prefix_pages, owner_start, slot_of, own_back, *returned, token, new_pool)
    return (result, new_pool)


def solution(mesh):
    in_specs = (
        P(("parts", "pool"), "tp"),
        P(None, "tp", ("parts", "pool"), None),
        P(None, "tp", ("parts", "pool"), None, None),
        P("parts"),
        P("parts"),
        P("parts", None, None),
    )
    out_specs = (P(("parts", "pool"), "tp"), P(None, "tp", ("parts", "pool"), None, None))
    return jax.shard_map(body, mesh=mesh, in_specs=in_specs, out_specs=out_specs, check_vma=False)
```

```python
import functools
import math

import jax
import jax.numpy as jnp
from jax import lax
from jax.experimental import pallas as pl
from jax.experimental.pallas import tpu as pltpu
from jax.sharding import PartitionSpec as P

HBM = pl.BlockSpec(memory_space=pl.ANY)
VMEM = pl.BlockSpec(memory_space=pltpu.VMEM)
SMEM = pl.BlockSpec(memory_space=pltpu.SMEM)
TILE = 256


def partner(index, step, groups):
    if groups & (groups - 1):
        return (index + step) % groups, (index + groups - step) % groups
    return index ^ step, index ^ step


def turn_of(index, source, groups):
    if groups & (groups - 1):
        return lax.rem(index + groups - source, groups)
    return index ^ source


def fetch_kernel(slots_ref, pool_ref, *rest):
    *sends, token_ref, sems = rest
    groups = slots_ref.shape[2]
    levels = sends[0].shape[0]
    me = lax.axis_index("pool")
    copies = []
    for step in range(groups - 1, -1, -1):
        dest = partner(me, step, groups)[0]
        for level in range(levels):
            slot = slots_ref[dest, level, me]
            copies.append(
                pltpu.make_async_copy(
                    pool_ref.at[:, :, slot], sends[step].at[level], sems.at[step, level]
                )
            )
    for copy in copies:
        copy.start()
    token_ref[0] = me
    for copy in copies:
        copy.wait()


def place_kernel(pages, length_ref, start_ref, slots_ref, *rest):
    backs, new_ref, sems = rest[:-4], rest[-2], rest[-1]
    _, levels, groups = slots_ref.shape
    me = lax.axis_index("pool")

    def each(act):
        for step in range(groups):
            request = partner(me, step, groups)[1]
            length = length_ref[request]
            first = lax.rem(start_ref[request] + length, groups)
            offset = lax.rem(me + groups - first, groups)

            @pl.when(offset < pages)
            def _():
                level = jnp.minimum(lax.div(length + offset, groups), levels - 1)
                slot = slots_ref[request, level, me]
                act(
                    pltpu.make_async_copy(backs[step], new_ref.at[:, :, slot], sems.at[step])
                )

    each(lambda copy: copy.start())
    each(lambda copy: copy.wait())


dot = functools.partial(lax.dot_general, preferred_element_type=jnp.float32)
ACROSS = (((1,), (1,)), ((), ()))
ALONG = (((1,), (0,)), ((), ()))


def staggered(items, scores_of, finish):
    ahead = scores_of(items[0])
    for place, item in enumerate(items):
        scores = ahead
        if place + 1 < len(items):
            ahead = scores_of(items[place + 1])
        finish(item, scores)


def suffix_kernel(
    scale, per_step, length_ref, start_ref, _, query_ref, suffix_ref, pool_ref, *rest
):
    mean_out, log_out, new_ref, *back_refs, means, logs, values, sem, sems = rest
    groups = len(back_refs)
    page_len, head_dim = pool_ref.shape[3:]
    suffix = query_ref.shape[0]
    pages = suffix // page_len
    head, step = pl.program_id(0), pl.program_id(1)
    copy = pltpu.make_async_copy(pool_ref, new_ref.at[:, pl.ds(head, 1)], sem)
    turn_now = head * pl.num_programs(1) + step

    def leaving(column):
        place = step * per_step + column
        return [
            pltpu.make_async_copy(means.at[column], mean_out.at[head, place], sems.at[0, column]),
            pltpu.make_async_copy(logs.at[column], log_out.at[head, place], sems.at[1, column]),
        ]

    def wait_leaving():
        for column in range(per_step):
            for part in leaving(column):
                part.wait()

    @pl.when(turn_now > 0)
    def _():
        wait_leaving()

    @pl.when(step == 0)
    def _():
        copy.start()
        values[:, pl.ds(0, head_dim)] = suffix_ref[1, 0]
        values[:, pl.ds(head_dim, head_dim)] = jnp.ones((suffix, head_dim), values.dtype)
        me = lax.axis_index("pool")
        first = lax.rem(start_ref[me] + length_ref[me], groups)
        for turn in range(groups):
            offset = lax.rem(partner(me, turn, groups)[0] + groups - first, groups)
            row = pl.multiple_of(jnp.minimum(offset, pages - 1) * page_len, page_len)
            for side in range(2):
                back_refs[turn][side, 0] = suffix_ref[side, 0, pl.ds(row, page_len), :]

    tile = min(TILE, suffix)
    seen = lax.broadcasted_iota(jnp.int32, (tile, tile), 1) <= lax.broadcasted_iota(
        jnp.int32, (tile, tile), 0
    )

    def scores_of(column):
        lanes = pl.ds(column * head_dim, head_dim)
        return [
            dot(query_ref[row:, lanes], suffix_ref[0, 0, pl.ds(row, tile), :], ACROSS)
            for row in range(0, suffix, tile)
        ]

    def finish(column, scores):
        scores = [
            [
                block[row : row + tile] if row else jnp.where(seen, block[:tile], -jnp.inf)
                for row in range(0, block.shape[0], tile)
            ]
            for block in scores
        ]
        blocks = len(scores)
        tops = [
            jnp.max(
                functools.reduce(jnp.maximum, [scores[key][row - key] for key in range(row + 1)]),
                axis=1,
                keepdims=True,
            )
            for row in range(blocks)
        ]
        mixed = [None] * blocks
        for key in range(blocks):
            weight = [
                jnp.exp2((scores[key][row - key] - tops[row]) * scale).astype(jnp.bfloat16)
                for row in range(key, blocks)
            ]
            weight = jnp.concatenate(weight, axis=0) if len(weight) > 1 else weight[0]
            part = dot(weight, values[pl.ds(key * tile, tile), :], ALONG)
            for row in range(key, blocks):
                piece = part[(row - key) * tile : (row - key + 1) * tile]
                mixed[row] = piece if mixed[row] is None else mixed[row] + piece
        for row in range(blocks):
            rows = pl.ds(row * tile, tile)
            count = mixed[row][:, head_dim:]
            means[column, rows, :] = mixed[row][:, :head_dim] / count
            logs[column, rows, :] = tops[row] * scale + jnp.log2(count)
        for part in leaving(column):
            part.start()

    staggered(range(per_step), scores_of, finish)

    @pl.when(step == pl.num_programs(1) - 1)
    def _():
        copy.wait()

    @pl.when(turn_now == pl.num_programs(0) * pl.num_programs(1) - 1)
    def _():
        wait_leaving()


def prefix_kernel(
    scale, per_step, length_ref, start_ref, query_ref, mean_ref, log_ref, *rest
):
    *page_refs, out_ref, token_ref, keys, values = rest
    groups = len(page_refs)
    levels, _, _, page_len, head_dim = page_refs[0].shape
    suffix = query_ref.shape[0]

    token_ref[...] = jnp.zeros_like(token_ref)

    @pl.when(pl.program_id(1) == 0)
    def _():
        me = lax.axis_index("pool")
        length, first = length_ref[me], start_ref[me]
        places = []
        for turn in range(groups):
            owner = partner(me, turn, groups)[1]
            for level in range(levels):
                rows = pl.ds((turn * levels + level) * page_len, page_len)
                seen = level * groups + lax.rem(owner + groups - first, groups) < length
                places.append((rows, seen))
                keys[rows, :] = page_refs[turn][level, 0, 0]

                @pl.when(seen)
                def _():
                    values[rows, pl.ds(0, head_dim)] = page_refs[turn][level, 1, 0]
                    values[rows, pl.ds(head_dim, head_dim)] = jnp.ones(
                        (page_len, head_dim), values.dtype
                    )

        page_zero = pl.ds(
            pl.multiple_of(turn_of(me, first, groups) * levels * page_len, page_len), page_len
        )
        for rows, seen in places:

            @pl.when(jnp.logical_not(seen))
            def _():
                keys[rows, :] = keys[page_zero, :]
                values[rows, :] = jnp.zeros((page_len, 2 * head_dim), values.dtype)

    def scores_of(column):
        query = query_ref[:, pl.ds(column * head_dim, head_dim)]
        return dot(query, keys[...], ACROSS)

    def finish(column, score):
        lanes = pl.ds(column * head_dim, head_dim)
        before = log_ref[0, column]
        top = jnp.maximum(before, jnp.max(score, axis=1, keepdims=True) * scale)
        weight = jnp.concatenate(
            [
                jnp.exp2(score[:, start : start + head_dim] * scale - top).astype(jnp.bfloat16)
                for start in range(0, score.shape[1], head_dim)
            ],
            axis=1,
        )
        mixed = dot(weight, values[...], ALONG)
        share = jnp.exp2(before - top)
        out_ref[:, lanes] = (
            (mixed[:, :head_dim] + mean_ref[0, column] * share) / (mixed[:, head_dim:] + share)
        ).astype(out_ref.dtype)

    staggered(range(per_step), scores_of, finish)


def body(queries, suffix_kv, pool_kv, prefix_pages, owner_start, page_slot):
    _, heads, slots, page_len, head_dim = pool_kv.shape
    _, groups, levels = page_slot.shape
    suffix = queries.shape[0]
    per_kv = queries.shape[1] // (heads * head_dim)
    pages = suffix // page_len
    fetched = -(-(levels * groups - pages) // groups)
    page = (2, heads, page_len, head_dim)
    slot_of = jnp.swapaxes(page_slot, 1, 2)
    dtype = pool_kv.dtype

    def exchange(sends):
        arrived = [None] * (groups - 1)
        for step in range(groups - 1, 0, -1):
            pairs = [(index, partner(index, step, groups)[0]) for index in range(groups)]
            arrived[step - 1] = lax.ppermute(sends[step - 1], "pool", pairs)
        return arrived

    own_pages, *sends, gathered = pl.pallas_call(
        fetch_kernel,
        out_shape=[pltpu.VMEM((fetched,) + page, dtype)] * groups
        + [jax.ShapeDtypeStruct((1,), jnp.int32)],
        in_specs=[SMEM, HBM],
        out_specs=[VMEM] * groups + [SMEM],
        scratch_shapes=[pltpu.SemaphoreType.DMA((groups, fetched))],
        name="gather_pages",
    )(slot_of, pool_kv)
    received = exchange(sends)

    per_step = math.gcd(per_kv, 8)
    steps = per_kv // per_step
    scale = math.log2(math.e) / math.sqrt(head_dim)

    def grant(size):
        return pltpu.CompilerParams(vmem_limit_bytes=size * 1024 * 1024)

    total = fetched * groups * page_len
    columns = pl.BlockSpec((suffix, per_step * head_dim), lambda h, s: (0, h * steps + s))
    per_head = pl.BlockSpec((1, per_step, suffix, head_dim), lambda h, s: (h, s, 0, 0))
    pages_of = pl.BlockSpec((fetched, 2, 1, page_len, head_dim), lambda h, s: (0, 0, h, 0, 0))

    def cost(keys):
        cells = heads * per_kv * suffix * keys
        return pl.CostEstimate(
            flops=6 * cells * head_dim, bytes_accessed=8 * queries.size, transcendentals=cells
        )

    means, logs, new_pool, own_back, *back_sends = pl.pallas_call(
        functools.partial(suffix_kernel, scale, per_kv),
        grid=(heads, 1),
        out_shape=[
            jax.ShapeDtypeStruct((heads, per_kv, suffix, head_dim), jnp.float32),
            jax.ShapeDtypeStruct((heads, per_kv, suffix, head_dim), jnp.float32),
            jax.ShapeDtypeStruct(pool_kv.shape, dtype),
        ]
        + [jax.ShapeDtypeStruct(page, dtype)] * groups,
        in_specs=[
            SMEM,
            SMEM,
            SMEM,
            pl.BlockSpec((suffix, per_kv * head_dim), lambda h, s: (0, h)),
            pl.BlockSpec((2, 1, suffix, head_dim), lambda h, s: (0, h, 0, 0)),
            pl.BlockSpec((2, 1, slots, page_len, head_dim), lambda h, s: (0, h, 0, 0, 0)),
        ],
        out_specs=[HBM, HBM, HBM]
        + [pl.BlockSpec((2, 1, page_len, head_dim), lambda h, s: (0, h, 0, 0))] * groups,
        scratch_shapes=[
            pltpu.VMEM((per_kv, suffix, head_dim), jnp.float32),
            pltpu.VMEM((per_kv, suffix, head_dim), jnp.float32),
            pltpu.VMEM((suffix, 2 * head_dim), dtype),
            pltpu.SemaphoreType.DMA(()),
            pltpu.SemaphoreType.DMA((2, per_kv)),
        ],
        compiler_params=grant(60),
        cost_estimate=cost(suffix),
        name="attend_suffix",
    )(prefix_pages, owner_start, gathered, queries, suffix_kv, pool_kv)
    returned = exchange(back_sends)

    result, token = pl.pallas_call(
        functools.partial(prefix_kernel, scale, per_step),
        grid=(heads, steps),
        out_shape=[
            jax.ShapeDtypeStruct(queries.shape, dtype),
            jax.ShapeDtypeStruct((8, head_dim), jnp.float32),
        ],
        in_specs=[
            SMEM,
            SMEM,
            columns,
            per_head,
            per_head,
        ]
        + [pages_of] * groups,
        out_specs=[columns, pl.BlockSpec((8, head_dim), lambda h, s: (0, 0))],
        scratch_shapes=[
            pltpu.VMEM((total, head_dim), dtype),
            pltpu.VMEM((total, 2 * head_dim), dtype),
        ],
        compiler_params=grant(52),
        cost_estimate=cost(total),
        name="attend_prefix",
    )(prefix_pages, owner_start, queries, means, logs, own_pages, *received)

    new_pool = pl.pallas_call(
        functools.partial(place_kernel, pages),
        out_shape=jax.ShapeDtypeStruct(pool_kv.shape, dtype),
        in_specs=[SMEM, SMEM, SMEM] + [VMEM] * groups + [HBM, HBM],
        out_specs=HBM,
        input_output_aliases={4 + groups: 0},
        scratch_shapes=[pltpu.SemaphoreType.DMA((groups,))],
        compiler_params=grant(50),
        name="place_pages",
    )(prefix_pages, owner_start, slot_of, own_back, *returned, token, new_pool)
    return (result, new_pool)


def solution(mesh):
    in_specs = (
        P(("parts", "pool"), "tp"),
        P(None, "tp", ("parts", "pool"), None),
        P(None, "tp", ("parts", "pool"), None, None),
        P("parts"),
        P("parts"),
        P("parts", None, None),
    )
    out_specs = (P(("parts", "pool"), "tp"), P(None, "tp", ("parts", "pool"), None, None))
    return jax.shard_map(body, mesh=mesh, in_specs=in_specs, out_specs=out_specs, check_vma=False)
```
